512 devices in a mesh: dp: 64 (over y_hi, z, core), tensor: 8 (over y_lo, x).
Axes of the slice: x: 4, y: 8 (y_hi: 4, y_lo: 2; y = y_hi * 2 + y_lo), z: 8, core: 2. Of those that a mesh axis runs over, the one named last changes fastest.
Arguments:
- q_base: bfloat16 [16384, 8192], P('dp', 'tensor'), may hold values from -48 to 48
- kv_base: bfloat16 [2, 16384, 1024], P(None, 'dp', 'tensor'), may hold values from -6 to 6
- cotangent: bfloat16 [16384, 8192], P('dp', 'tensor'), may hold values from -6 to 6
- steering: float32 [8192], P('dp'), may hold values from -6 to 6
- w_query: bfloat16 [8192, 8192], P('dp', 'tensor'), may hold values from -0.0625 to 0.0625
- w_kv: bfloat16 [2, 8192, 1024], P(None, 'dp', 'tensor'), may hold values from -0.0625 to 0.0625
- prompt_cache: bfloat16 [2, 32, 1024, 1024], P(None, None, 'dp', 'tensor'), may hold values from -6 to 6
- prompt_ids: int32 [64], P('dp'), may hold values from 0 to 31
- dialogue_lens: int32 [64], P('dp'), may hold values from 64 to 256, as said below
- prompt_lens: int32 [32], replicated, may hold values from 256 to 1024, as said below
Outputs:
- query_grad: bfloat16 [16384, 8192], P('dp', 'tensor')
- kv_grad: bfloat16 [2, 16384, 1024], P(None, 'dp', 'tensor')
- steer_grad: float32 [8192], P('dp')
The draws below stay inside these ranges and needn't reach their ends.
Inputs may be any that keep to these rules, and one draw needn't show every extreme that they name: `dialogue_lens`: some dialogue has all 256 tokens live. `prompt_lens`: some prompt has all 1024 positions live.
All inputs are finite; a program needn't handle non-finite values.
Results may differ from the reference program's by a relative error of at most 0.0121.
Values may be sent and summed in bfloat16 or wider, within the bound.
No kernel may reach another device: no remote copies, remote signals or barrier semaphores. Data moves between devices by JAX's collectives and lax.ppermute only.
A program may use at most 64 MiB of HBM per device.

```python
import math
import jax
import jax.numpy as jnp
import numpy as np
from jax import lax

D = 8192
HEADS = 64
KVH = 8
HD = 128
PROMPTS = 32
PL = 1024
LEN = 256
DIALOGUES = 64
TOKENS = 16384


def shared_normals(key):
    first, second = jax.random.split(key)
    queries = jax.random.truncated_normal(first, -6.0, 6.0, (TOKENS, HEADS * HD), jnp.float32)
    kv_pair = jax.random.truncated_normal(second, -6.0, 6.0, (2, TOKENS, KVH * HD), jnp.float32)
    return (queries, kv_pair)


def draw_kv_base(key, part):
    queries, kv_pair = shared_normals(key)
    return kv_pair.astype(jnp.bfloat16)


def draw_q_base(key, part):
    queries, kv_pair = shared_normals(key)
    return queries.astype(jnp.bfloat16)


def draw_dialogue_lens(key, part):
    key = jax.random.fold_in(key, 7)
    first, second = jax.random.split(key)
    lengths = jax.random.randint(first, (DIALOGUES,), LEN // 4, LEN + 1, jnp.int32)
    fullest = jax.random.randint(second, (), 0, DIALOGUES, jnp.int32)
    return jnp.where(jnp.arange(DIALOGUES, dtype=jnp.int32) == fullest, LEN, lengths).astype(jnp.int32)


def draw_prompt_lens(key, part):
    key = jax.random.fold_in(key, 9)
    first, second = jax.random.split(key)
    lengths = jax.random.randint(first, (PROMPTS,), PL // 4, PL + 1, jnp.int32)
    fullest = jax.random.randint(second, (), 0, PROMPTS, jnp.int32)
    return jnp.where(jnp.arange(PROMPTS, dtype=jnp.int32) == fullest, PL, lengths).astype(jnp.int32)


def with_ends(entries, rng, least, top_value):
    index_at = [jax.random.randint(jax.random.fold_in(rng, axis), (), 0, length) for axis, length in enumerate(entries.shape)]
    widest = entries.shape.index(max(entries.shape))
    beside = index_at[:widest] + [(index_at[widest] + 1) % entries.shape[widest]] + index_at[widest + 1:]
    return entries.at[tuple(index_at)].set(least).at[tuple(beside)].set(top_value)


def block_scale(key, dims, cuts, least, largest):
    level = 1.0
    for axis_at, blocks in cuts:
        steps = jax.random.uniform(jax.random.fold_in(jax.random.fold_in(key, 6), axis_at), (blocks,), jnp.float32, least / len(cuts), largest / len(cuts))
        level = level * jnp.repeat(jnp.exp(steps), dims[axis_at] // blocks).reshape((-1,) + (1,) * (len(dims) - 1 - axis_at))
    return level


def rank_table(count, slope):
    loads = [(1 << 20) // math.isqrt(rank ** slope) + 1 for rank in range(1, count + 1)]
    spread = 1 + sum(loads) // (1 << 30)
    return np.cumsum(np.array([max(1, weight // spread) for weight in loads]))


def ranked(stream_key, dims, amount, skew):
    table = rank_table(amount, skew)
    pick = jax.random.randint(jax.random.fold_in(stream_key, 1), dims, 0, int(table[amount - 1]))
    grade = jnp.searchsorted(jnp.asarray(table, jnp.int32), pick, side="right")
    return jax.random.permutation(jax.random.fold_in(stream_key, 2), amount)[grade].astype(jnp.int32)


def scatter_about(stream_key, shape, spread, limit, cuts=(), kind=jnp.bfloat16):
    factor_of = block_scale(stream_key, shape, cuts, -0.22, 0.18) if cuts else 1.0
    result = jax.random.normal(stream_key, shape, jnp.float32) * spread * factor_of
    return jnp.minimum(jnp.maximum(result, -limit), limit).astype(kind)


def setup_inputs(seed: int = 0) -> dict:
    streams_of = jax.random.split(jax.random.key(seed), 11)
    q_base = draw_q_base(jax.random.fold_in(streams_of[10], 71), 0)
    kv_base = draw_kv_base(jax.random.fold_in(streams_of[10], 71), 0)
    cotangent = scatter_about(streams_of[2], (TOKENS, HEADS * HD), 1.0, 6.0, ((0, 64), (1, 8)))
    steering = scatter_about(streams_of[3], (D,), 1.0, 6.0, ((0, 64),), jnp.float32)
    w_query = scatter_about(streams_of[4], (D, HEADS * HD), D ** -0.5, 0.0625, ((0, 64), (1, 8)))
    w_kv = scatter_about(streams_of[5], (2, D, KVH * HD), D ** -0.5, 0.0625, ((1, 64), (2, 8)))
    prompt_cache = scatter_about(streams_of[6], (2, PROMPTS, PL, KVH * HD), 1.0, 6.0, ((2, 64), (3, 8)))
    prompt_ids = with_ends(ranked(streams_of[7], (DIALOGUES,), PROMPTS, 2), jax.random.fold_in(streams_of[7], 3), 0, PROMPTS - 1).astype(jnp.int32)
    dialogue_lens = draw_dialogue_lens(jax.random.fold_in(streams_of[10], 71), 0)
    prompt_lens = draw_prompt_lens(jax.random.fold_in(streams_of[10], 71), 0)
    return dict(q_base=q_base, kv_base=kv_base, cotangent=cotangent, steering=steering, w_query=w_query, w_kv=w_kv, prompt_cache=prompt_cache, prompt_ids=prompt_ids, dialogue_lens=dialogue_lens, prompt_lens=prompt_lens)


def scores_of(queries, pre_keys, own_keys, pre_mask, own_mask, score_scale):
    pre_scores = jnp.einsum('tgd,pd->tgp', queries.astype(jnp.float32), pre_keys.astype(jnp.float32)) * score_scale
    own_scores = jnp.einsum('tgd,ud->tgu', queries.astype(jnp.float32), own_keys.astype(jnp.float32)) * score_scale
    pre_scores = jnp.where(pre_mask[None, None, :], pre_scores, -jnp.inf)
    own_scores = jnp.where(own_mask[:, None, :], own_scores, -jnp.inf)
    return (pre_scores, own_scores)

def statistics(pre_scores, own_scores):
    maxima = jnp.maximum(lax.optimization_barrier(jnp.max(pre_scores, -1)), lax.optimization_barrier(jnp.max(own_scores, -1)))
    totals = lax.optimization_barrier(jnp.sum(jnp.exp(pre_scores - maxima[..., None]), -1)) + lax.optimization_barrier(jnp.sum(jnp.exp(own_scores - maxima[..., None]), -1))
    return (maxima, totals)

def backward_of(queries, pre_keys, pre_values, own_keys, own_values, grad_out, pre_scores, own_scores, maxima, totals, score_scale):
    pre_probs = jnp.exp(pre_scores - maxima[..., None]) / totals[..., None]
    own_probs = jnp.exp(own_scores - maxima[..., None]) / totals[..., None]
    pre_weights = pre_probs.astype(jnp.bfloat16).astype(jnp.float32)
    own_weights = own_probs.astype(jnp.bfloat16).astype(jnp.float32)
    pre_v = pre_values.astype(jnp.float32)
    own_v = own_values.astype(jnp.float32)
    attended = jnp.einsum('tgp,pd->tgd', pre_weights, pre_v) + jnp.einsum('tgu,ud->tgd', own_weights, own_v)
    grad_float = grad_out.astype(jnp.float32)
    delta = lax.optimization_barrier(jnp.sum(grad_float * attended, -1))
    pre_gw = jnp.einsum('tgd,pd->tgp', grad_float, pre_v)
    own_gw = jnp.einsum('tgd,ud->tgu', grad_float, own_v)
    pre_gs = (pre_probs * (pre_gw - delta[..., None]) * score_scale).astype(jnp.bfloat16).astype(jnp.float32)
    own_gs = (own_probs * (own_gw - delta[..., None]) * score_scale).astype(jnp.bfloat16).astype(jnp.float32)
    grad_query = jnp.einsum('tgp,pd->tgd', pre_gs, pre_keys.astype(jnp.float32)) + jnp.einsum('tgu,ud->tgd', own_gs, own_keys.astype(jnp.float32))
    grad_key = jnp.einsum('tgu,tgd->ud', own_gs, queries.astype(jnp.float32))
    grad_value = jnp.einsum('tgu,tgd->ud', own_weights, grad_float)
    return (grad_query, grad_key, grad_value)

def reference(q_base, kv_base, cotangent, steering, w_query, w_kv, prompt_cache, prompt_ids, dialogue_lens, prompt_lens):
    precise = lax.Precision.HIGHEST
    shift_q = jnp.dot(steering, w_query.astype(jnp.float32), precision=precise)
    shift_kv = jnp.einsum('d,cdk->ck', steering, w_kv.astype(jnp.float32), precision=precise)
    query = (q_base.astype(jnp.float32) + shift_q[None, :]).astype(jnp.bfloat16)
    keys_values = (kv_base.astype(jnp.float32) + shift_kv[:, None, :]).astype(jnp.bfloat16)
    group_size = HEADS // KVH
    score_scale = 1.0 / math.sqrt(HD)

    def one_dialogue(dialog):
        row_start = (dialog * LEN).astype(jnp.int32)
        queries = lax.dynamic_slice_in_dim(query, row_start, LEN, 0).reshape(LEN, KVH, group_size, HD)
        own_kv = lax.dynamic_slice_in_dim(keys_values, row_start, LEN, 1).reshape(2, LEN, KVH, HD)
        grads = lax.dynamic_slice_in_dim(cotangent, row_start, LEN, 0).reshape(LEN, KVH, group_size, HD)
        live = dialogue_lens[dialog]
        prompt = prompt_ids[dialog]
        prompt_live = prompt_lens[prompt]
        prefix = lax.dynamic_index_in_dim(prompt_cache, prompt, 1, keepdims=False).reshape(2, PL, KVH, HD)
        places = jnp.arange(LEN, dtype=jnp.int32)
        grads = jnp.where((places < live)[:, None, None, None], grads, jnp.zeros_like(grads))
        own_mask = (places[None, :] <= places[:, None]) & (places[None, :] < live)
        pre_mask = jnp.arange(PL, dtype=jnp.int32) < prompt_live

        def one_head(head_index):
            q_head = lax.dynamic_index_in_dim(queries, head_index, 1, keepdims=False)
            g_head = lax.dynamic_index_in_dim(grads, head_index, 1, keepdims=False)
            p_head = lax.dynamic_index_in_dim(prefix, head_index, 2, keepdims=False)
            o_head = lax.dynamic_index_in_dim(own_kv, head_index, 2, keepdims=False)
            pre_scores, own_scores = scores_of(q_head, p_head[0], o_head[0], pre_mask, own_mask, score_scale)
            maxima, totals = statistics(pre_scores, own_scores)
            return backward_of(q_head, p_head[0], p_head[1], o_head[0], o_head[1], g_head, pre_scores, own_scores, maxima, totals, score_scale)
        grad_query, grad_key, grad_value = lax.map(one_head, jnp.arange(KVH, dtype=jnp.int32))
        grad_query = grad_query.transpose(1, 0, 2, 3).reshape(LEN, HEADS * HD)
        grad_key = grad_key.transpose(1, 0, 2).reshape(LEN, KVH * HD)
        grad_value = grad_value.transpose(1, 0, 2).reshape(LEN, KVH * HD)
        return (grad_query, grad_key, grad_value)
    grad_query, grad_key, grad_value = lax.map(one_dialogue, jnp.arange(DIALOGUES, dtype=jnp.int32))
    grad_query = grad_query.reshape(TOKENS, HEADS * HD)
    kv_full = jnp.stack([grad_key.reshape(TOKENS, KVH * HD), grad_value.reshape(TOKENS, KVH * HD)])
    query_sum = lax.optimization_barrier(jnp.sum(grad_query, 0))
    kv_sum = lax.optimization_barrier(jnp.sum(kv_full, 1))
    steer_grad = jnp.dot(w_query.astype(jnp.float32), query_sum, precision=precise) + jnp.einsum('cdk,ck->d', w_kv.astype(jnp.float32), kv_sum, precision=precise)
    return (grad_query.astype(jnp.bfloat16), kv_full.astype(jnp.bfloat16), steer_grad)
```

```python
import functools
import math

import jax
import jax.numpy as jnp
from jax import lax
from jax.experimental import pallas as pl
from jax.experimental.pallas import tpu as pltpu
from jax.sharding import PartitionSpec as P

HD = 128
NN = (((1,), (0,)), ((), ()))
NT = (((1,), (1,)), ((), ()))
TN = (((0,), (0,)), ((), ()))
VMEM = pl.BlockSpec(memory_space=pltpu.VMEM)
SMEM = pl.BlockSpec(memory_space=pltpu.SMEM)
PARAMS = pltpu.CompilerParams(vmem_limit_bytes=40 * 2**20)


def dot(a, b, dims):
    return lax.dot_general(a, b, dims, preferred_element_type=jnp.float32)


def in_thirds(row):
    first = row.astype(jnp.bfloat16).astype(jnp.float32)
    second = (row - first).astype(jnp.bfloat16).astype(jnp.float32)
    third = row - first - second
    rest = jnp.zeros((13, row.shape[1]), jnp.float32)
    return jnp.concatenate([first, second, third, rest], axis=0).astype(jnp.bfloat16)


def project_kernel(prompt_id, steering, w_query, w_kv, message):
    thirds = in_thirds(steering[...])
    parts = [
        jnp.sum(dot(thirds, weights, NN), 0, keepdims=True)
        for weights in (w_query[...], w_kv[0], w_kv[1])
    ]
    mark = jnp.full((1, HD), prompt_id[0], jnp.int32).astype(jnp.float32)
    row = jnp.concatenate(parts + [mark], axis=1)
    for peer in range(message.shape[0]):
        message[peer] = row


def pick_kernel(ids, cache, outgoing):
    def one(peer, carry):
        outgoing[peer] = cache[:, ids[peer]]
        return carry

    lax.fori_loop(0, outgoing.shape[0], one, 0, unroll=4)


def attend_kernel(
    ids,
    lens,
    prompt_lens,
    arrived,
    q_ref,
    kv_ref,
    cot_ref,
    shifts,
    dq_ref,
    dkv_ref,
    message,
    keys,
    values,
    grad_keys,
    grad_values,
    sums,
):
    span = arrived.shape[0] * arrived.shape[2]
    own = kv_ref.shape[1]
    heads = q_ref.shape[1] // HD
    scale = 1.0 / math.sqrt(HD)
    to_log2 = scale * math.log2(math.e)
    live = lens[0]
    prompt_live = prompt_lens[ids[0]]
    total = shifts[0]
    for peer in range(1, shifts.shape[0]):
        total = total + shifts[peer]

    def shift_of(chunk):
        return total[:, chunk * HD : (chunk + 1) * HD]

    for head in range(heads):
        sums[head] = shift_of(head)
    keys[:span] = arrived[:, 0].reshape(span, HD)
    values[:span] = arrived[:, 1].reshape(span, HD)
    keys[span:] = (kv_ref[0].astype(jnp.float32) + shift_of(heads)).astype(jnp.bfloat16)
    values[span:] = (kv_ref[1].astype(jnp.float32) + shift_of(heads + 1)).astype(jnp.bfloat16)
    grad_keys[...] = jnp.zeros_like(grad_keys)
    grad_values[...] = jnp.zeros_like(grad_values)

    def one_head(head, carry):
        columns = pl.ds(pl.multiple_of(head * HD, HD), HD)
        query = (q_ref[:, columns].astype(jnp.float32) + sums[head]).astype(jnp.bfloat16)
        token = lax.broadcasted_iota(jnp.int32, (own, HD), 0)
        grad = cot_ref[:, columns].astype(jnp.float32)
        grad = jnp.where(token < live, grad, 0.0).astype(jnp.bfloat16)
        scores = dot(query, keys[...], NT)
        place = lax.broadcasted_iota(jnp.int32, (own, span), 1)
        pre = jnp.where(place < prompt_live, scores[:, :span], -jnp.inf)
        key_at = lax.broadcasted_iota(jnp.int32, (own, own), 1)
        token_at = lax.broadcasted_iota(jnp.int32, (own, own), 0)
        admitted = (key_at <= token_at) & (key_at < live)
        mine = jnp.where(admitted, scores[:, span:], -jnp.inf)
        top = jnp.maximum(jnp.max(pre, 1, keepdims=True), jnp.max(mine, 1, keepdims=True))
        top = top * to_log2
        pre = jnp.exp2(pre * to_log2 - top)
        mine = jnp.exp2(mine * to_log2 - top)
        mass = jnp.sum(pre, 1, keepdims=True) + jnp.sum(mine, 1, keepdims=True)
        grad_weights = dot(grad, values[...], NT)
        pre_gw, mine_gw = grad_weights[:, :span], grad_weights[:, span:]
        inverse = 1.0 / mass
        delta = jnp.sum(pre * pre_gw, 1, keepdims=True) + jnp.sum(mine * mine_gw, 1, keepdims=True)
        slope = scale * inverse
        offset = delta * inverse * slope
        pre_gs = (pre * (pre_gw * slope - offset)).astype(jnp.bfloat16)
        mine_gs = (mine * (mine_gw * slope - offset)).astype(jnp.bfloat16)
        weights = (mine * inverse).astype(jnp.bfloat16)
        grad_query = dot(pre_gs, keys[:span], NN) + dot(mine_gs, keys[span:], NN)
        dq_ref[:, columns] = grad_query.astype(jnp.bfloat16)
        grad_keys[...] += dot(mine_gs, query, TN)
        grad_values[...] += dot(weights, grad, TN)
        sums[head] = jnp.sum(grad_query, 0, keepdims=True)
        return carry

    lax.fori_loop(0, heads, one_head, 0)
    dkv_ref[0] = grad_keys[...].astype(jnp.bfloat16)
    dkv_ref[1] = grad_values[...].astype(jnp.bfloat16)
    row = jnp.concatenate(
        [sums[head] for head in range(heads)]
        + [jnp.sum(grad_keys[...], 0, keepdims=True), jnp.sum(grad_values[...], 0, keepdims=True)],
        axis=1,
    )
    for peer in range(message.shape[0]):
        message[peer] = row


def steer_kernel(sums, w_query, w_kv, message):
    total = sums[0]
    for peer in range(1, sums.shape[0]):
        total = total + sums[peer]
    wide = w_query.shape[1]
    part = dot(in_thirds(total[:, :wide]), w_query[...], NT)
    for c in range(2):
        chunk = total[:, wide + c * HD : wide + (c + 1) * HD]
        part = part + dot(in_thirds(chunk), w_kv[c], NT)
    row = jnp.sum(part, 0, keepdims=True)
    for peer in range(message.shape[0]):
        message[peer] = row


def shards(
    q_base,
    kv_base,
    cotangent,
    steering,
    w_query,
    w_kv,
    prompt_cache,
    prompt_ids,
    dialogue_lens,
    prompt_lens,
):
    dp = lax.axis_size("dp")
    tensor = lax.axis_size("tensor")
    f32 = jnp.float32
    tokens, width = q_base.shape
    positions = prompt_cache.shape[2]
    all_width = width + 2 * HD
    message = pl.pallas_call(
        project_kernel,
        out_shape=jax.ShapeDtypeStruct((dp, 1, all_width + HD), f32),
        in_specs=[SMEM, VMEM, VMEM, VMEM],
        out_specs=VMEM,
        compiler_params=PARAMS,
        name="project",
    )(prompt_ids, steering.reshape(1, -1), w_query, w_kv)
    shares = lax.all_to_all(message, "dp", 0, 0, tiled=True)
    ids = shares[:, 0, all_width].astype(jnp.int32)
    outgoing = pl.pallas_call(
        pick_kernel,
        out_shape=jax.ShapeDtypeStruct((dp, 2, positions, HD), jnp.bfloat16),
        in_specs=[SMEM, VMEM],
        out_specs=VMEM,
        compiler_params=PARAMS,
        name="pick",
    )(ids, prompt_cache)
    arrived = lax.all_to_all(outgoing, "dp", 0, 0, tiled=True)
    keys_held = dp * positions + tokens
    query_grad, kv_grad, message = pl.pallas_call(
        attend_kernel,
        out_shape=(
            jax.ShapeDtypeStruct(q_base.shape, jnp.bfloat16),
            jax.ShapeDtypeStruct(kv_base.shape, jnp.bfloat16),
            jax.ShapeDtypeStruct((dp, 1, all_width), f32),
        ),
        in_specs=[SMEM, SMEM, SMEM, VMEM, VMEM, VMEM, VMEM, VMEM],
        out_specs=(VMEM, VMEM, VMEM),
        scratch_shapes=[
            pltpu.VMEM((keys_held, HD), jnp.bfloat16),
            pltpu.VMEM((keys_held, HD), jnp.bfloat16),
            pltpu.VMEM((tokens, HD), f32),
            pltpu.VMEM((tokens, HD), f32),
            pltpu.VMEM((width // HD, 1, HD), f32),
        ],
        compiler_params=PARAMS,
        name="attend",
    )(prompt_ids, dialogue_lens, prompt_lens, arrived, q_base, kv_base, cotangent, shares)
    sums = lax.all_to_all(message, "dp", 0, 0, tiled=True)
    message = pl.pallas_call(
        steer_kernel,
        out_shape=jax.ShapeDtypeStruct((tensor, 1, steering.shape[0]), f32),
        in_specs=[VMEM, VMEM, VMEM],
        out_specs=VMEM,
        compiler_params=PARAMS,
        name="steer",
    )(sums, w_query, w_kv)
    parts = lax.all_to_all(message, "tensor", 0, 0, tiled=True)
    return (query_grad, kv_grad, jnp.sum(parts, axis=(0, 1)))


def solution(mesh):
    placed = (
        P("dp", "tensor"),
        P(None, "dp", "tensor"),
        P("dp", "tensor"),
        P("dp"),
        P("dp", "tensor"),
        P(None, "dp", "tensor"),
        P(None, None, "dp", "tensor"),
        P("dp"),
        P("dp"),
        P(),
    )
    return jax.shard_map(
        shards,
        mesh=mesh,
        in_specs=placed,
        out_specs=(P("dp", "tensor"), P(None, "dp", "tensor"), P("dp")),
        check_vma=False,
    )
```

```python
import functools
import math

import jax
import jax.numpy as jnp
from jax import lax
from jax.experimental import pallas as pl
from jax.experimental.pallas import tpu as pltpu
from jax.sharding import PartitionSpec as P

HD = 128
ROWS = 16
MASKED = -1e30
NN = (((1,), (0,)), ((), ()))
NT = (((1,), (1,)), ((), ()))
TN = (((0,), (0,)), ((), ()))
VMEM = pl.BlockSpec(memory_space=pltpu.VMEM)
HBM = pl.BlockSpec(memory_space=pltpu.HBM)
SMEM = pl.BlockSpec(memory_space=pltpu.SMEM)
PARAMS = pltpu.CompilerParams(vmem_limit_bytes=40 * 2**20)


def dot(a, b, dims):
    return lax.dot_general(a, b, dims, preferred_element_type=jnp.float32)


def in_thirds(row):
    first = row.astype(jnp.bfloat16).astype(jnp.float32)
    second = (row - first).astype(jnp.bfloat16).astype(jnp.float32)
    third = row - first - second
    rest = jnp.zeros((13, row.shape[1]), jnp.float32)
    return jnp.concatenate([first, second, third, rest], axis=0).astype(jnp.bfloat16)


def in_halves(chunks):
    half = len(chunks) // 2
    rows = [jnp.concatenate(chunks[:half], axis=1), jnp.concatenate(chunks[half:], axis=1)]
    return jnp.concatenate(rows, axis=0).astype(jnp.bfloat16)


def summed(blocks):
    total = blocks[0].astype(jnp.float32)
    for peer in range(1, blocks.shape[0]):
        total = total + blocks[peer].astype(jnp.float32)
    return total


def chunk_of(halves, chunk, count):
    row, at = divmod(chunk, count // 2)
    return halves[row : row + 1, at * HD : (at + 1) * HD]


def project_kernel(prompt_id, steering, w_query, w_kv, message, vector, wq, wkv, sems):
    copies = [
        pltpu.make_async_copy(source, held, sems.at[at])
        for at, (source, held) in enumerate(((w_query, wq), (steering, vector), (w_kv, wkv)))
    ]
    for copy in copies:
        copy.start()
    mark = jnp.full((1, HD), prompt_id[0], jnp.int32).astype(jnp.float32)
    for copy in copies:
        copy.wait()
    thirds = in_thirds(vector[...])
    parts = [jnp.sum(dot(thirds, w[...], NN), 0, keepdims=True) for w in (wq, wkv.at[0], wkv.at[1])]
    row = jnp.concatenate(parts, axis=1)
    chunks = [row[:, at : at + HD] for at in range(0, row.shape[1], HD)]
    half = len(chunks) // 2
    block = in_halves(chunks[:half] + [mark] + chunks[half:] + [mark])
    for peer in range(message.shape[0]):
        message[peer] = block


def pick_kernel(shares, cache, outgoing, marks, ids, sems):
    peers = shares.shape[0]
    last = shares.shape[2] - HD
    lane = lax.broadcasted_iota(jnp.int32, (2, HD), 1)
    found = jnp.zeros((2, HD), jnp.float32)
    for peer in range(peers):
        found = jnp.where(lane == peer, shares[peer, :, last:].astype(jnp.float32), found)
    marks[...] = found[:1].astype(jnp.int32)
    copy = pltpu.make_async_copy(marks, ids, sems.at[0])
    copy.start()
    copy.wait()
    for peer in range(peers):
        pltpu.make_async_copy(cache.at[:, ids[0, peer]], outgoing.at[peer], sems.at[1]).start()
    pltpu.make_async_copy(outgoing, outgoing, sems.at[1]).wait()


def attend_kernel(
    ids,
    lens,
    prompt_lens,
    arrived,
    q_ref,
    kv_ref,
    cot_ref,
    shifts,
    dq_ref,
    dkv_ref,
    message,
    keys,
    keys_t,
    values_t,
    grad_keys,
    grad_values,
    causal,
    scores0,
    scores1,
    slopes0,
    slopes1,
    grads0,
    grads1,
    weights0,
    weights1,
    queries0,
    queries1,
    outs0,
    outs1,
    factors0,
    factors1,
):
    f32, bf16 = jnp.float32, jnp.bfloat16
    span = arrived.shape[0] * arrived.shape[2]
    own = kv_ref.shape[1]
    heads = q_ref.shape[1] // HD
    scale = 1.0 / math.sqrt(HD)
    to_log2 = scale * math.log2(math.e)
    live = lens[0]
    prompt_live = prompt_lens[ids[0]]
    total = summed(shifts)
    shift = [chunk_of(total[:, : total.shape[1] - HD], c, heads + 2) for c in range(heads + 2)]
    pre_keys = arrived[:, 0].reshape(span, HD)
    pre_values = arrived[:, 1].reshape(span, HD)
    own_keys = (kv_ref[0].astype(f32) + shift[heads]).astype(bf16)
    own_values = (kv_ref[1].astype(f32) + shift[heads + 1]).astype(bf16)
    keys[:span] = pre_keys
    keys[span:] = own_keys
    keys_t[:HD, :span] = pre_keys.T
    keys_t[:HD, span:] = own_keys.T
    values_t[:, :span] = pre_values.T
    values_t[:, span:] = own_values.T
    feature = lax.broadcasted_iota(jnp.int32, (HD, span + own), 0)
    place = lax.broadcasted_iota(jnp.int32, (HD, span + own), 1)
    barred = jnp.where((place >= prompt_live) & (place < span), MASKED, 0.0)
    keys_t[HD:] = jnp.where(feature == HD - 1, barred, keys_t[:HD].astype(f32)).astype(bf16)
    token_at = lax.broadcasted_iota(jnp.int32, (own, own), 0)
    key_at = lax.broadcasted_iota(jnp.int32, (own, own), 1)
    causal[...] = jnp.where((key_at <= token_at) & (key_at < live), 0.0, MASKED)
    grad_keys[...] = jnp.zeros_like(grad_keys)
    grad_values[...] = jnp.zeros_like(grad_values)
    token = lax.broadcasted_iota(jnp.int32, (own, HD), 0)
    lane = lax.broadcasted_iota(jnp.int32, (own, HD), 1)
    scores, slopes = (scores0, scores1), (slopes0, slopes1)
    grads, weights = (grads0, grads1), (weights0, weights1)
    queries, outs, factors = (queries0, queries1), (outs0, outs1), (factors0, factors1)
    sums = []

    def products(head):
        slot, columns = head % 2, slice(head * HD, (head + 1) * HD)
        query = (q_ref[:, columns].astype(f32) + shift[head]).astype(bf16)
        grad = jnp.where(token < live, cot_ref[:, columns].astype(f32), 0.0).astype(bf16)
        queries[slot][...] = query
        outs[slot][...] = grad
        scaled = query.astype(f32) * to_log2
        high = scaled.astype(bf16)
        low = jnp.where(lane == HD - 1, 1.0, scaled - high.astype(f32)).astype(bf16)
        scores[slot][...] = dot(jnp.concatenate([high, low], axis=1), keys_t[...], NN)
        slopes[slot][...] = dot(grad, values_t[...], NN)

    def softmax(head):
        slot = head % 2
        for at in range(0, own, ROWS):
            rows = slice(at, at + ROWS)
            score = scores[slot][rows]
            score = jnp.concatenate([score[:, :span], score[:, span:] + causal[rows]], axis=1)
            prob = jnp.exp2(score - jnp.max(score, 1, keepdims=True))
            slope = slopes[slot][rows]
            inverse = 1.0 / jnp.sum(prob, 1, keepdims=True)
            delta = jnp.sum(prob * slope, 1, keepdims=True) * inverse
            grads[slot][rows] = (prob * (slope - delta)).astype(bf16)
            weights[slot][rows] = (prob[:, span:] * inverse).astype(bf16)
            factors[slot][rows] = jnp.broadcast_to(inverse * scale, (ROWS, HD))

    def gradients(head):
        slot, columns = head % 2, slice(head * HD, (head + 1) * HD)
        factor = factors[slot][...]
        grad_query = dot(grads[slot][...], keys[...], NN) * factor
        dq_ref[:, columns] = grad_query.astype(bf16)
        sums.append(jnp.sum(grad_query, 0, keepdims=True))
        query = (queries[slot][...].astype(f32) * factor).astype(bf16)
        grad_keys[...] += dot(grads[slot][:, span:], query, TN)
        grad_values[...] += dot(weights[slot][...], outs[slot][...], TN)

    products(0)
    for head in range(heads):
        if head > 0:
            gradients(head - 1)
        if head + 1 < heads:
            products(head + 1)
        softmax(head)
    gradients(heads - 1)
    dkv_ref[0] = grad_keys[...].astype(bf16)
    dkv_ref[1] = grad_values[...].astype(bf16)
    last = [jnp.sum(grad_keys[...], 0, keepdims=True), jnp.sum(grad_values[...], 0, keepdims=True)]
    block = in_halves(sums + last)
    for peer in range(message.shape[0]):
        message[peer] = block


def steer_kernel(sums, w_query, w_kv, message):
    total = summed(sums)
    heads = w_query.shape[1] // HD
    chunks = [chunk_of(total, chunk, heads + 2) for chunk in range(heads + 2)]
    part = dot(in_thirds(jnp.concatenate(chunks[:heads], axis=1)), w_query[...], NT)
    for c in range(2):
        part = part + dot(in_thirds(chunks[heads + c]), w_kv[c], NT)
    row = jnp.sum(part, 0, keepdims=True)
    for peer in range(message.shape[0]):
        message[peer] = row


def shards(
    q_base,
    kv_base,
    cotangent,
    steering,
    w_query,
    w_kv,
    prompt_cache,
    prompt_ids,
    dialogue_lens,
    prompt_lens,
):
    dp = lax.axis_size("dp")
    tensor = lax.axis_size("tensor")
    f32 = jnp.float32
    tokens, width = q_base.shape
    positions = prompt_cache.shape[2]
    half_width = (width + 2 * HD) // 2
    bf16 = jnp.bfloat16
    message = pl.pallas_call(
        project_kernel,
        out_shape=jax.ShapeDtypeStruct((dp, 2, half_width + HD), bf16),
        in_specs=[SMEM, HBM, HBM, HBM],
        out_specs=VMEM,
        scratch_shapes=[
            pltpu.VMEM((1, steering.shape[0]), f32),
            pltpu.VMEM(w_query.shape, bf16),
            pltpu.VMEM(w_kv.shape, bf16),
            pltpu.SemaphoreType.DMA((3,)),
        ],
        compiler_params=pltpu.CompilerParams(vmem_limit_bytes=63 * 2**20),
        name="project",
    )(prompt_ids, steering.reshape(1, -1), w_query, w_kv)
    shares = lax.all_to_all(message, "dp", 0, 0, tiled=True)
    outgoing = pl.pallas_call(
        pick_kernel,
        out_shape=jax.ShapeDtypeStruct((dp, 2, positions, HD), bf16),
        in_specs=[VMEM, VMEM],
        out_specs=HBM,
        scratch_shapes=[
            pltpu.VMEM((1, HD), jnp.int32),
            pltpu.SMEM((1, HD), jnp.int32),
            pltpu.SemaphoreType.DMA((2,)),
        ],
        compiler_params=PARAMS,
        name="pick",
    )(shares, prompt_cache)
    arrived = lax.all_to_all(outgoing, "dp", 0, 0, tiled=True)
    keys_held = dp * positions + tokens
    query_grad, kv_grad, message = pl.pallas_call(
        attend_kernel,
        out_shape=(
            jax.ShapeDtypeStruct(q_base.shape, jnp.bfloat16),
            jax.ShapeDtypeStruct(kv_base.shape, jnp.bfloat16),
            jax.ShapeDtypeStruct((dp, 2, half_width), bf16),
        ),
        in_specs=[SMEM, SMEM, SMEM, VMEM, VMEM, VMEM, VMEM, VMEM],
        out_specs=(VMEM, VMEM, VMEM),
        scratch_shapes=[
            pltpu.VMEM((keys_held, HD), bf16),
            pltpu.VMEM((2 * HD, keys_held), bf16),
            pltpu.VMEM((HD, keys_held), bf16),
            pltpu.VMEM((tokens, HD), f32),
            pltpu.VMEM((tokens, HD), f32),
            pltpu.VMEM((tokens, tokens), f32),
        ]
        + [
            pltpu.VMEM((tokens, columns), kind)
            for columns, kind in (
                (keys_held, f32),
                (keys_held, f32),
                (keys_held, bf16),
                (tokens, bf16),
                (HD, bf16),
                (HD, bf16),
                (HD, f32),
            )
            for slot in range(2)
        ],
        compiler_params=PARAMS,
        name="attend",
    )(prompt_ids, dialogue_lens, prompt_lens, arrived, q_base, kv_base, cotangent, shares)
    sums = lax.all_to_all(message, "dp", 0, 0, tiled=True)
    message = pl.pallas_call(
        steer_kernel,
        out_shape=jax.ShapeDtypeStruct((tensor, 1, steering.shape[0]), f32),
        in_specs=[VMEM, VMEM, VMEM],
        out_specs=VMEM,
        compiler_params=PARAMS,
        name="steer",
    )(sums, w_query, w_kv)
    parts = lax.all_to_all(message, "tensor", 0, 0, tiled=True)
    return (query_grad, kv_grad, jnp.sum(parts, axis=(0, 1)))


def solution(mesh):
    placed = (
        P("dp", "tensor"),
        P(None, "dp", "tensor"),
        P("dp", "tensor"),
        P("dp"),
        P("dp", "tensor"),
        P(None, "dp", "tensor"),
        P(None, None, "dp", "tensor"),
        P("dp"),
        P("dp"),
        P(),
    )
    return jax.shard_map(
        shards,
        mesh=mesh,
        in_specs=placed,
        out_specs=(P("dp", "tensor"), P(None, "dp", "tensor"), P("dp")),
        check_vma=False,
    )
```

```python
import functools
import math

import jax
import jax.numpy as jnp
from jax import lax
from jax.experimental import pallas as pl
from jax.experimental.pallas import tpu as pltpu
from jax.sharding import PartitionSpec as P

HD = 128
ROWS = 32
TILE = 256
MASKED = -1e30
NN = (((1,), (0,)), ((), ()))
NT = (((1,), (1,)), ((), ()))
TN = (((0,), (0,)), ((), ()))
VMEM = pl.BlockSpec(memory_space=pltpu.VMEM)
HBM = pl.BlockSpec(memory_space=pltpu.HBM)
SMEM = pl.BlockSpec(memory_space=pltpu.SMEM)
PARAMS = pltpu.CompilerParams(vmem_limit_bytes=40 * 2**20)


def dot(a, b, dims):
    return lax.dot_general(a, b, dims, preferred_element_type=jnp.float32)


def in_thirds(row):
    first = row.astype(jnp.bfloat16).astype(jnp.float32)
    second = (row - first).astype(jnp.bfloat16).astype(jnp.float32)
    third = row - first - second
    rest = jnp.zeros((13, row.shape[1]), jnp.float32)
    return jnp.concatenate([first, second, third, rest], axis=0).astype(jnp.bfloat16)


def in_halves(chunks):
    half = len(chunks) // 2
    rows = [jnp.concatenate(chunks[:half], axis=1), jnp.concatenate(chunks[half:], axis=1)]
    return jnp.concatenate(rows, axis=0)


def summed(blocks):
    total = blocks[0].astype(jnp.float32)
    for peer in range(1, blocks.shape[0]):
        total = total + blocks[peer].astype(jnp.float32)
    return total


def chunk_of(halves, chunk, count):
    row, at = divmod(chunk, count // 2)
    return halves[row : row + 1, at * HD : (at + 1) * HD]


def project_kernel(prompt_id, steering, w_query, w_kv, message, vector, wq, wkv, sems):
    copies = [
        pltpu.make_async_copy(source, held, sems.at[at])
        for at, (source, held) in enumerate(((w_query, wq), (steering, vector), (w_kv, wkv)))
    ]
    for copy in copies:
        copy.start()
    mark = jnp.full((1, HD), prompt_id[0], jnp.int32)
    for copy in copies:
        copy.wait()
    thirds = in_thirds(vector[...])
    parts = [jnp.sum(dot(thirds, w[...], NN), 0, keepdims=True) for w in (wq, wkv.at[0], wkv.at[1])]
    row = jnp.concatenate(parts, axis=1)
    peak = jnp.max(jnp.abs(row), 1, keepdims=True)
    power = jnp.clip(jnp.floor(14.9 - jnp.log2(peak)), -60.0, 60.0)
    whole = jnp.floor(row * jnp.exp2(power) + 0.5).astype(jnp.int32)
    scale = jnp.broadcast_to(power, (1, HD)).astype(jnp.int32)
    chunks = [whole[:, at : at + HD] for at in range(0, whole.shape[1], HD)]
    half = len(chunks) // 2
    block = in_halves(chunks[:half] + [mark] + chunks[half:] + [scale]).astype(jnp.int16)
    for peer in range(message.shape[0]):
        message[peer] = block


def shifts_from(shares):
    last = shares.shape[2] - HD
    total = jnp.zeros((2, last), jnp.float32)
    for peer in range(shares.shape[0]):
        block = shares[peer].astype(jnp.int32).astype(jnp.float32)
        scale = jnp.exp2(-block[1:, last:])
        total = total + block[:, :last] * jnp.concatenate([scale] * (last // HD), axis=1)
    return total


def pick_kernel(shares, cache, outgoing, marks, ids, sems):
    peers = shares.shape[0]
    last = shares.shape[2] - HD
    lane = lax.broadcasted_iota(jnp.int32, (2, HD), 1)
    found = jnp.zeros((2, HD), jnp.int32)
    for peer in range(peers):
        found = jnp.where(lane == peer, shares[peer, :, last:].astype(jnp.int32), found)
    marks[...] = found[:1]
    copy = pltpu.make_async_copy(marks, ids, sems.at[0])
    copy.start()
    copy.wait()
    for peer in range(peers):
        pltpu.make_async_copy(cache.at[:, ids[0, peer]], outgoing.at[peer], sems.at[1]).start()
    pltpu.make_async_copy(outgoing, outgoing, sems.at[1]).wait()


def attend_kernel(
    ids,
    lens,
    prompt_lens,
    arrived,
    q_ref,
    kv_ref,
    cot_ref,
    shifts,
    dq_ref,
    dkv_ref,
    message,
    keys,
    keys_t,
    values_t,
    grad_keys,
    grad_values,
    causal,
    scores0,
    scores1,
    slopes0,
    slopes1,
    grads0,
    grads1,
    weights0,
    weights1,
    factors0,
    factors1,
    queries,
    outs,
):
    f32, bf16 = jnp.float32, jnp.bfloat16
    span = arrived.shape[0] * arrived.shape[2]
    own = kv_ref.shape[1]
    heads = q_ref.shape[1] // HD
    scale = 1.0 / math.sqrt(HD)
    to_log2 = scale * math.log2(math.e)
    live = lens[0]
    prompt_live = prompt_lens[ids[0]]
    total = shifts_from(shifts)
    shift = [chunk_of(total, chunk, heads + 2) for chunk in range(heads + 2)]
    pre_keys = arrived[:, 0].reshape(span, HD)
    pre_values = arrived[:, 1].reshape(span, HD)
    own_keys = (kv_ref[0].astype(f32) + shift[heads]).astype(bf16)
    own_values = (kv_ref[1].astype(f32) + shift[heads + 1]).astype(bf16)
    keys[:span] = pre_keys
    keys[span:] = own_keys
    keys_t[:HD, :span] = pre_keys.T
    keys_t[:HD, span:] = own_keys.T
    values_t[:, :span] = pre_values.T
    values_t[:, span:] = own_values.T
    feature = lax.broadcasted_iota(jnp.int32, (HD, span + own), 0)
    place = lax.broadcasted_iota(jnp.int32, (HD, span + own), 1)
    barred = jnp.where((place >= prompt_live) & (place < span), MASKED, 0.0)
    keys_t[HD:] = jnp.where(feature == HD - 1, barred, keys_t[:HD].astype(f32)).astype(bf16)
    token_at = lax.broadcasted_iota(jnp.int32, (own, own), 0)
    key_at = lax.broadcasted_iota(jnp.int32, (own, own), 1)
    causal[...] = jnp.where((key_at <= token_at) & (key_at < live), 0.0, MASKED)
    grad_keys[...] = jnp.zeros_like(grad_keys)
    grad_values[...] = jnp.zeros_like(grad_values)
    token = lax.broadcasted_iota(jnp.int32, (own, HD), 0)
    lane = lax.broadcasted_iota(jnp.int32, (own, HD), 1)
    scores, slopes = (scores0, scores1), (slopes0, slopes1)
    grads, weights = (grads0, grads1), (weights0, weights1)
    factors = (factors0, factors1)
    sums = []
    tiles = (span + own) // TILE

    def operands(head):
        columns = slice(head * HD, (head + 1) * HD)
        query = (q_ref[:, columns].astype(f32) + shift[head]).astype(bf16)
        grad = jnp.where(token < live, cot_ref[:, columns].astype(f32), 0.0).astype(bf16)
        queries[:, columns] = query
        outs[:, columns] = grad
        scaled = query.astype(f32) * to_log2
        high = scaled.astype(bf16)
        low = jnp.where(lane == HD - 1, 1.0, scaled - high.astype(f32)).astype(bf16)
        return jnp.concatenate([high, low], axis=1), grad

    def product(head, at, query, grad):
        slot, part = head % 2, slice(at % tiles * TILE, (at % tiles + 1) * TILE)
        if at < tiles:
            scores[slot][:, part] = dot(query, keys_t[:, part], NN)
        else:
            slopes[slot][:, part] = dot(grad, values_t[:, part], NN)

    def softmax(head, at):
        slot, rows = head % 2, slice(at * ROWS, (at + 1) * ROWS)
        score = scores[slot][rows]
        score = jnp.concatenate([score[:, :span], score[:, span:] + causal[rows]], axis=1)
        prob = jnp.exp2(score - jnp.max(score, 1, keepdims=True))
        slope = slopes[slot][rows]
        inverse = 1.0 / jnp.sum(prob, 1, keepdims=True)
        delta = jnp.sum(prob * slope, 1, keepdims=True) * inverse
        grads[slot][rows] = (prob * (slope - delta)).astype(bf16)
        weights[slot][rows] = (prob[:, span:] * inverse).astype(bf16)
        factors[slot][rows] = jnp.broadcast_to(inverse * scale, (ROWS, HD))

    def gradient(head, at, total):
        slot, columns = head % 2, slice(head * HD, (head + 1) * HD)
        if at < tiles:
            part = slice(at * TILE, (at + 1) * TILE)
            term = dot(grads[slot][:, part], keys[part], NN)
            return term if total is None else total + term
        if at == tiles:
            factor = factors[slot][...]
            total = total * factor
            dq_ref[:, columns] = total.astype(bf16)
            sums.append(jnp.sum(total, 0, keepdims=True))
            query = (queries[:, columns].astype(f32) * factor).astype(bf16)
            grad_keys[...] += dot(grads[slot][:, span:], query, TN)
        else:
            grad_values[...] += dot(weights[slot][...], outs[:, columns], TN)
        return total

    current = operands(0)
    for at in range(2 * tiles):
        product(0, at, *current)
    chunks = own // ROWS
    for head in range(heads):
        if head + 1 < heads:
            current = operands(head + 1)
        total, done, made = None, 0, 0
        for chunk in range(chunks):
            while head + 1 < heads and made < 2 * tiles * (chunk + 1) // chunks:
                product(head + 1, made, *current)
                made += 1
            while head > 0 and done < (tiles + 2) * (chunk + 1) // chunks:
                total = gradient(head - 1, done, total)
                done += 1
            softmax(head, chunk)
    total = None
    for at in range(tiles + 2):
        total = gradient(heads - 1, at, total)
    dkv_ref[0] = grad_keys[...].astype(bf16)
    dkv_ref[1] = grad_values[...].astype(bf16)
    last = [jnp.sum(grad_keys[...], 0, keepdims=True), jnp.sum(grad_values[...], 0, keepdims=True)]
    block = in_halves(sums + last).astype(bf16)
    for peer in range(message.shape[0]):
        message[peer] = block


def steer_kernel(sums, w_query, w_kv, message):
    total = summed(sums)
    heads = w_query.shape[1] // HD
    chunks = [chunk_of(total, chunk, heads + 2) for chunk in range(heads + 2)]
    part = dot(in_thirds(jnp.concatenate(chunks[:heads], axis=1)), w_query[...], NT)
    for c in range(2):
        part = part + dot(in_thirds(chunks[heads + c]), w_kv[c], NT)
    row = jnp.sum(part, 0, keepdims=True)
    for peer in range(message.shape[0]):
        message[peer] = row


def shards(
    q_base,
    kv_base,
    cotangent,
    steering,
    w_query,
    w_kv,
    prompt_cache,
    prompt_ids,
    dialogue_lens,
    prompt_lens,
):
    dp = lax.axis_size("dp")
    tensor = lax.axis_size("tensor")
    f32 = jnp.float32
    tokens, width = q_base.shape
    positions = prompt_cache.shape[2]
    half_width = (width + 2 * HD) // 2
    bf16 = jnp.bfloat16
    message = pl.pallas_call(
        project_kernel,
        out_shape=jax.ShapeDtypeStruct((dp, 2, half_width + HD), jnp.int16),
        in_specs=[SMEM, HBM, HBM, HBM],
        out_specs=VMEM,
        scratch_shapes=[
            pltpu.VMEM((1, steering.shape[0]), f32),
            pltpu.VMEM(w_query.shape, bf16),
            pltpu.VMEM(w_kv.shape, bf16),
            pltpu.SemaphoreType.DMA((3,)),
        ],
        compiler_params=pltpu.CompilerParams(vmem_limit_bytes=63 * 2**20),
        name="project",
    )(prompt_ids, steering.reshape(1, -1), w_query, w_kv)
    shares = lax.all_to_all(message, "dp", 0, 0, tiled=True)
    outgoing = pl.pallas_call(
        pick_kernel,
        out_shape=jax.ShapeDtypeStruct((dp, 2, positions, HD), bf16),
        in_specs=[VMEM, VMEM],
        out_specs=HBM,
        scratch_shapes=[
            pltpu.VMEM((1, HD), jnp.int32),
            pltpu.SMEM((1, HD), jnp.int32),
            pltpu.SemaphoreType.DMA((2,)),
        ],
        compiler_params=PARAMS,
        name="pick",
    )(shares, prompt_cache)
    arrived = lax.all_to_all(outgoing, "dp", 0, 0, tiled=True)
    keys_held = dp * positions + tokens
    query_grad, kv_grad, message = pl.pallas_call(
        attend_kernel,
        out_shape=(
            jax.ShapeDtypeStruct(q_base.shape, jnp.bfloat16),
            jax.ShapeDtypeStruct(kv_base.shape, jnp.bfloat16),
            jax.ShapeDtypeStruct((dp, 2, half_width), bf16),
        ),
        in_specs=[SMEM, SMEM, SMEM, VMEM, VMEM, VMEM, VMEM, VMEM],
        out_specs=(VMEM, VMEM, VMEM),
        scratch_shapes=[
            pltpu.VMEM((keys_held, HD), bf16),
            pltpu.VMEM((2 * HD, keys_held), bf16),
            pltpu.VMEM((HD, keys_held), bf16),
            pltpu.VMEM((tokens, HD), f32),
            pltpu.VMEM((tokens, HD), f32),
            pltpu.VMEM((tokens, tokens), f32),
        ]
        + [
            pltpu.VMEM((tokens, columns), kind)
            for columns, kind in (
                (keys_held, f32),
                (keys_held, f32),
                (keys_held, bf16),
                (tokens, bf16),
                (HD, f32),
            )
            for slot in range(2)
        ]
        + [pltpu.VMEM(q_base.shape, bf16), pltpu.VMEM(q_base.shape, bf16)],
        compiler_params=PARAMS,
        name="attend",
    )(prompt_ids, dialogue_lens, prompt_lens, arrived, q_base, kv_base, cotangent, shares)
    sums = lax.all_to_all(message, "dp", 0, 0, tiled=True)
    message = pl.pallas_call(
        steer_kernel,
        out_shape=jax.ShapeDtypeStruct((tensor, 1, steering.shape[0]), f32),
        in_specs=[VMEM, VMEM, VMEM],
        out_specs=VMEM,
        compiler_params=PARAMS,
        name="steer",
    )(sums, w_query, w_kv)
    parts = lax.all_to_all(message, "tensor", 0, 0, tiled=True)
    return (query_grad, kv_grad, jnp.sum(parts, axis=(0, 1)))


def solution(mesh):
    placed = (
        P("dp", "tensor"),
        P(None, "dp", "tensor"),
        P("dp", "tensor"),
        P("dp"),
        P("dp", "tensor"),
        P(None, "dp", "tensor"),
        P(None, None, "dp", "tensor"),
        P("dp"),
        P("dp"),
        P(),
    )
    return jax.shard_map(
        shards,
        mesh=mesh,
        in_specs=placed,
        out_specs=(P("dp", "tensor"), P(None, "dp", "tensor"), P("dp")),
        check_vma=False,
    )
```

```python
import functools
import math

import jax
import jax.numpy as jnp
from jax import lax
from jax.experimental import pallas as pl
from jax.experimental.pallas import tpu as pltpu
from jax.sharding import PartitionSpec as P

HD = 128
ROWS = 32
TILE = 256
MASKED = -1e30
NN = (((1,), (0,)), ((), ()))
NT = (((1,), (1,)), ((), ()))
TN = (((0,), (0,)), ((), ()))
VMEM = pl.BlockSpec(memory_space=pltpu.VMEM)
HBM = pl.BlockSpec(memory_space=pltpu.HBM)
SMEM = pl.BlockSpec(memory_space=pltpu.SMEM)
PARAMS = pltpu.CompilerParams(vmem_limit_bytes=40 * 2**20)


def dot(a, b, dims):
    return lax.dot_general(a, b, dims, preferred_element_type=jnp.float32)


def in_thirds(row):
    first = row.astype(jnp.bfloat16).astype(jnp.float32)
    second = (row - first).astype(jnp.bfloat16).astype(jnp.float32)
    third = row - first - second
    rest = jnp.zeros((13, row.shape[1]), jnp.float32)
    return jnp.concatenate([first, second, third, rest], axis=0).astype(jnp.bfloat16)


def in_halves(chunks):
    half = len(chunks) // 2
    rows = [jnp.concatenate(chunks[:half], axis=1), jnp.concatenate(chunks[half:], axis=1)]
    return jnp.concatenate(rows, axis=0)


def summed(blocks):
    total = blocks[0].astype(jnp.float32)
    for peer in range(1, blocks.shape[0]):
        total = total + blocks[peer].astype(jnp.float32)
    return total


def chunk_of(halves, chunk, count):
    row, at = divmod(chunk, count // 2)
    return halves[row : row + 1, at * HD : (at + 1) * HD]


def project_kernel(prompt_id, steering, w_query, w_kv, message, vector, wq, wkv, sems):
    copies = [
        pltpu.make_async_copy(source, held, sems.at[at])
        for at, (source, held) in enumerate(((w_query, wq), (steering, vector), (w_kv, wkv)))
    ]
    for copy in copies:
        copy.start()
    mark = jnp.full((1, HD), prompt_id[0], jnp.int32)
    for copy in copies:
        copy.wait()
    thirds = in_thirds(vector[...])
    parts = [jnp.sum(dot(thirds, w[...], NN), 0, keepdims=True) for w in (wq, wkv.at[0], wkv.at[1])]
    row = jnp.concatenate(parts, axis=1)
    peak = jnp.max(jnp.abs(row), 1, keepdims=True)
    power = jnp.clip(jnp.floor(14.9 - jnp.log2(peak)), -60.0, 60.0)
    whole = jnp.floor(row * jnp.exp2(power) + 0.5).astype(jnp.int32)
    scale = jnp.broadcast_to(power, (1, HD)).astype(jnp.int32)
    chunks = [whole[:, at : at + HD] for at in range(0, whole.shape[1], HD)]
    half = len(chunks) // 2
    block = in_halves(chunks[:half] + [mark] + chunks[half:] + [scale]).astype(jnp.int16)
    for peer in range(message.shape[0]):
        message[peer] = block


def shifts_from(shares):
    last = shares.shape[2] - HD
    total = jnp.zeros((2, last), jnp.float32)
    for peer in range(shares.shape[0]):
        block = shares[peer].astype(jnp.int32).astype(jnp.float32)
        scale = jnp.exp2(-block[1:, last:])
        total = total + block[:, :last] * jnp.concatenate([scale] * (last // HD), axis=1)
    return total


def pick_kernel(shares, cache, outgoing, marks, ids, sems):
    peers = shares.shape[0]
    last = shares.shape[2] - HD
    lane = lax.broadcasted_iota(jnp.int32, (2, HD), 1)
    found = jnp.zeros((2, HD), jnp.int32)
    for peer in range(peers):
        found = jnp.where(lane == peer, shares[peer, :, last:].astype(jnp.int32), found)
    marks[...] = found[:1]
    copy = pltpu.make_async_copy(marks, ids, sems.at[0])
    copy.start()
    copy.wait()
    for peer in range(peers):
        pltpu.make_async_copy(cache.at[:, ids[0, peer]], outgoing.at[peer], sems.at[1]).start()
    pltpu.make_async_copy(outgoing, outgoing, sems.at[1]).wait()


def two_parts(query):
    scaled = query.astype(jnp.float32) * (math.log2(math.e) / math.sqrt(HD))
    high = scaled.astype(jnp.bfloat16)
    lane = lax.broadcasted_iota(jnp.int32, query.shape, 1)
    low = jnp.where(lane == HD - 1, 1.0, scaled - high.astype(jnp.float32)).astype(jnp.bfloat16)
    return jnp.concatenate([high, low], axis=1)


def column(block, at):
    lane = lax.broadcasted_iota(jnp.int32, block.shape, 1)
    return jnp.sum(jnp.where(lane == at, block, 0.0), 1, keepdims=True)


def fill_own(live, keys, keys_two, causal):
    lane = lax.broadcasted_iota(jnp.int32, keys.shape, 1)
    keys_two[:, :HD] = keys
    keys_two[:, HD:] = jnp.where(lane == HD - 1, 0.0, keys.astype(jnp.float32)).astype(jnp.bfloat16)
    token_at = lax.broadcasted_iota(jnp.int32, causal.shape, 0)
    key_at = lax.broadcasted_iota(jnp.int32, causal.shape, 1)
    causal[...] = jnp.where((key_at <= token_at) & (key_at < live), 0.0, MASKED)


def shift_kernel(lens, shares, q_ref, kv_ref, cot_ref, outgoing, queries, outs, own):
    del outgoing
    f32, bf16 = jnp.float32, jnp.bfloat16
    heads = q_ref.shape[1] // HD
    total = shifts_from(shares)
    shift = [chunk_of(total, chunk, heads + 2) for chunk in range(heads + 2)]
    for c in range(2):
        own[c] = (kv_ref[c].astype(f32) + shift[heads + c]).astype(bf16)
    token = lax.broadcasted_iota(jnp.int32, (q_ref.shape[0], HD), 0)
    for head in range(heads):
        columns = slice(head * HD, (head + 1) * HD)
        queries[:, columns] = (q_ref[:, columns].astype(f32) + shift[head]).astype(bf16)
        grad = jnp.where(token < lens[0], cot_ref[:, columns].astype(f32), 0.0)
        outs[:, columns] = grad.astype(bf16)


def prepare_kernel(
    ids, prompt_lens, lens, queries, outs, own, stats, sloped, plain, keys_two, causal
):
    f32, bf16 = jnp.float32, jnp.bfloat16
    heads = queries.shape[1] // HD
    fill_own(lens[0], own[0], keys_two, causal)
    prompt_live = jnp.full((queries.shape[0], 1), prompt_lens[ids[0]], jnp.int32)
    stats[:, 3 * heads : 3 * heads + 1] = prompt_live.astype(f32)
    for head in range(heads):
        columns = slice(head * HD, (head + 1) * HD)
        score = dot(two_parts(queries[:, columns]), keys_two[...], NT) + causal[...]
        top = jnp.max(score, 1, keepdims=True)
        prob = jnp.exp2(score - top)
        slope = prob * dot(outs[:, columns], own[1], NT)
        stats[:, head : head + 1] = top
        stats[:, heads + head : heads + head + 1] = jnp.sum(prob, 1, keepdims=True)
        stats[:, 2 * heads + head : 2 * heads + head + 1] = jnp.sum(slope, 1, keepdims=True)
        sloped[head] = dot(slope.astype(bf16), own[0], NN).astype(bf16)
        plain[head] = dot(prob.astype(bf16), own[0], NN).astype(bf16)


def attend_kernel(
    arrived,
    queries,
    outs,
    stats,
    sloped,
    plain,
    dq_ref,
    message,
    final,
    keys,
    keys_t,
    values_t,
    scores0,
    scores1,
    slopes0,
    slopes1,
    grads0,
    grads1,
    factors0,
    factors1,
    terms0,
    terms1,
):
    f32, bf16 = jnp.float32, jnp.bfloat16
    span = arrived.shape[0] * arrived.shape[2]
    tokens = queries.shape[0]
    heads = queries.shape[1] // HD
    scale = 1.0 / math.sqrt(HD)
    keys[...] = arrived[:, 0].reshape(span, HD)
    keys_t[:HD] = arrived[:, 0].reshape(span, HD).T
    values_t[...] = arrived[:, 1].reshape(span, HD).T
    feature = lax.broadcasted_iota(jnp.int32, (HD, span), 0)
    prompt_live = jnp.broadcast_to(column(stats[:8], 3 * heads), (8, HD))[:1]
    prompt_live = jnp.concatenate([prompt_live] * (span // HD), axis=1)
    place = lax.broadcasted_iota(jnp.int32, (1, span), 1).astype(f32)
    barred = jnp.where(place >= prompt_live, MASKED, 0.0)
    keys_t[HD:] = jnp.where(feature == HD - 1, barred, keys_t[:HD].astype(f32)).astype(bf16)
    scores, slopes = (scores0, scores1), (slopes0, slopes1)
    grads, factors, terms = (grads0, grads1), (factors0, factors1), (terms0, terms1)
    query_sums, key_sums, value_sums = [], [], []
    tiles = span // TILE

    def columns(head):
        return slice(head * HD, (head + 1) * HD)

    def product(head, at, query):
        slot, part = head % 2, slice(at % tiles * TILE, (at % tiles + 1) * TILE)
        if at < tiles:
            scores[slot][:, part] = dot(query, keys_t[:, part], NN)
        else:
            slopes[slot][:, part] = dot(outs[:, columns(head)], values_t[:, part], NN)

    def softmax(head, at):
        slot, rows = head % 2, slice(at * ROWS, (at + 1) * ROWS)
        own_top, own_mass, own_slope = (column(stats[rows], n * heads + head) for n in range(3))
        score = scores[slot][rows]
        top = jnp.maximum(jnp.max(score, 1, keepdims=True), own_top)
        prob = jnp.exp2(score - top)
        share = jnp.exp2(own_top - top)
        slope = slopes[slot][rows]
        inverse = 1.0 / (jnp.sum(prob, 1, keepdims=True) + own_mass * share)
        delta = (jnp.sum(prob * slope, 1, keepdims=True) + own_slope * share) * inverse
        grads[slot][rows] = (prob * (slope - delta)).astype(bf16)
        factor = inverse * scale
        factors[slot][rows] = jnp.broadcast_to(factor, (ROWS, HD))
        own_factor = factor * share
        term = sloped[head, rows].astype(f32) - delta * plain[head, rows].astype(f32)
        terms[slot][rows] = term * own_factor
        by_query = (own_slope - delta * own_mass) * own_factor
        by_out = own_mass * share * inverse
        key_sums.append(by_query * queries[rows, columns(head)].astype(f32))
        value_sums.append(by_out * outs[rows, columns(head)].astype(f32))
        for n, value in enumerate((top, inverse, delta)):
            final[rows, n * heads + head : n * heads + head + 1] = value

    def gradient(head, at, total):
        slot = head % 2
        if at < tiles:
            part = slice(at * TILE, (at + 1) * TILE)
            term = dot(grads[slot][:, part], keys[part], NN)
            return term if total is None else total + term
        total = total * factors[slot][...] + terms[slot][...]
        dq_ref[:, columns(head)] = total.astype(bf16)
        query_sums.append(jnp.sum(total, 0, keepdims=True))
        return total

    query = two_parts(queries[:, columns(0)])
    for at in range(2 * tiles):
        product(0, at, query)
    chunks = tokens // ROWS
    for head in range(heads):
        if head + 1 < heads:
            query = two_parts(queries[:, columns(head + 1)])
        total, done, made = None, 0, 0
        for chunk in range(chunks):
            while head + 1 < heads and made < 2 * tiles * (chunk + 1) // chunks:
                product(head + 1, made, query)
                made += 1
            while head > 0 and done < (tiles + 1) * (chunk + 1) // chunks:
                total = gradient(head - 1, done, total)
                done += 1
            softmax(head, chunk)
    total = None
    for at in range(tiles + 1):
        total = gradient(heads - 1, at, total)
    last = [jnp.sum(sum(rows), 0, keepdims=True) for rows in (key_sums, value_sums)]
    block = in_halves(query_sums + last).astype(bf16)
    for peer in range(message.shape[0]):
        message[peer] = block


def finish_kernel(lens, queries, outs, own, final, dkv_ref, token, keys_two, causal):
    bf16 = jnp.bfloat16
    heads = queries.shape[1] // HD
    fill_own(lens[0], own[0], keys_two, causal)
    grad_keys = grad_values = None
    for head in range(heads):
        columns = slice(head * HD, (head + 1) * HD)
        top, inverse, delta = (column(final[...], n * heads + head) for n in range(3))
        query, grad = queries[:, columns], outs[:, columns]
        score = dot(two_parts(query), keys_two[...], NT) + causal[...]
        prob = jnp.exp2(score - top) * inverse
        mine = (prob * (dot(grad, own[1], NT) - delta) * (1.0 / math.sqrt(HD))).astype(bf16)
        by_key = dot(mine, query, TN)
        by_value = dot(prob.astype(bf16), grad, TN)
        grad_keys = by_key if head == 0 else grad_keys + by_key
        grad_values = by_value if head == 0 else grad_values + by_value
    dkv_ref[0] = grad_keys.astype(bf16)
    dkv_ref[1] = grad_values.astype(bf16)
    token[...] = jnp.zeros_like(token)


def steer_kernel(sums, w_query, w_kv, token, message):
    del token
    total = summed(sums)
    heads = w_query.shape[1] // HD
    chunks = [chunk_of(total, chunk, heads + 2) for chunk in range(heads + 2)]
    part = dot(in_thirds(jnp.concatenate(chunks[:heads], axis=1)), w_query[...], NT)
    for c in range(2):
        part = part + dot(in_thirds(chunks[heads + c]), w_kv[c], NT)
    row = jnp.sum(part, 0, keepdims=True)
    for peer in range(message.shape[0]):
        message[peer] = row


def shards(
    q_base,
    kv_base,
    cotangent,
    steering,
    w_query,
    w_kv,
    prompt_cache,
    prompt_ids,
    dialogue_lens,
    prompt_lens,
):
    dp = lax.axis_size("dp")
    tensor = lax.axis_size("tensor")
    f32 = jnp.float32
    tokens, width = q_base.shape
    positions = prompt_cache.shape[2]
    half_width = (width + 2 * HD) // 2
    bf16 = jnp.bfloat16
    message = pl.pallas_call(
        project_kernel,
        out_shape=jax.ShapeDtypeStruct((dp, 2, half_width + HD), jnp.int16),
        in_specs=[SMEM, HBM, HBM, HBM],
        out_specs=VMEM,
        scratch_shapes=[
            pltpu.VMEM((1, steering.shape[0]), f32),
            pltpu.VMEM(w_query.shape, bf16),
            pltpu.VMEM(w_kv.shape, bf16),
            pltpu.SemaphoreType.DMA((3,)),
        ],
        compiler_params=pltpu.CompilerParams(vmem_limit_bytes=63 * 2**20),
        name="project",
    )(prompt_ids, steering.reshape(1, -1), w_query, w_kv)
    shares = lax.all_to_all(message, "dp", 0, 0, tiled=True)
    outgoing = pl.pallas_call(
        pick_kernel,
        out_shape=jax.ShapeDtypeStruct((dp, 2, positions, HD), bf16),
        in_specs=[VMEM, VMEM],
        out_specs=HBM,
        scratch_shapes=[
            pltpu.VMEM((1, HD), jnp.int32),
            pltpu.SMEM((1, HD), jnp.int32),
            pltpu.SemaphoreType.DMA((2,)),
        ],
        compiler_params=PARAMS,
        name="pick",
    )(shares, prompt_cache)
    arrived = lax.all_to_all(outgoing, "dp", 0, 0, tiled=True)
    heads = width // HD
    span = dp * positions
    by_head = jax.ShapeDtypeStruct((heads, tokens, HD), bf16)
    by_row = jax.ShapeDtypeStruct((tokens, HD), f32)
    own_scratch = [pltpu.VMEM((tokens, 2 * HD), bf16), pltpu.VMEM((tokens, tokens), f32)]
    queries, outs, own = pl.pallas_call(
        shift_kernel,
        out_shape=(
            jax.ShapeDtypeStruct((tokens, width), bf16),
            jax.ShapeDtypeStruct((tokens, width), bf16),
            jax.ShapeDtypeStruct((2, tokens, HD), bf16),
        ),
        in_specs=[SMEM, VMEM, VMEM, VMEM, VMEM, HBM],
        out_specs=(VMEM,) * 3,
        compiler_params=PARAMS,
        name="shift",
    )(dialogue_lens, shares, q_base, kv_base, cotangent, outgoing)
    stats, sloped, plain = pl.pallas_call(
        prepare_kernel,
        out_shape=(by_row, by_head, by_head),
        in_specs=[SMEM, SMEM, SMEM, VMEM, VMEM, VMEM],
        out_specs=(VMEM,) * 3,
        scratch_shapes=own_scratch,
        compiler_params=PARAMS,
        name="prepare",
    )(prompt_ids, prompt_lens, dialogue_lens, queries, outs, own)
    query_grad, message, final = pl.pallas_call(
        attend_kernel,
        out_shape=(
            jax.ShapeDtypeStruct(q_base.shape, bf16),
            jax.ShapeDtypeStruct((dp, 2, half_width), bf16),
            by_row,
        ),
        in_specs=[VMEM] * 6,
        out_specs=(VMEM, VMEM, VMEM),
        scratch_shapes=[
            pltpu.VMEM((span, HD), bf16),
            pltpu.VMEM((2 * HD, span), bf16),
            pltpu.VMEM((HD, span), bf16),
        ]
        + [
            pltpu.VMEM((tokens, columns), kind)
            for columns, kind in ((span, f32), (span, f32), (span, bf16), (HD, f32), (HD, f32))
            for slot in range(2)
        ],
        compiler_params=PARAMS,
        name="attend",
    )(arrived, queries, outs, stats, sloped, plain)
    kv_grad, token = pl.pallas_call(
        finish_kernel,
        out_shape=(
            jax.ShapeDtypeStruct(kv_base.shape, bf16),
            jax.ShapeDtypeStruct((8, HD), f32),
        ),
        in_specs=[SMEM] + [VMEM] * 4,
        out_specs=(VMEM, VMEM),
        scratch_shapes=own_scratch,
        compiler_params=PARAMS,
        name="finish",
    )(dialogue_lens, queries, outs, own, final)
    sums = lax.all_to_all(message, "dp", 0, 0, tiled=True)
    message = pl.pallas_call(
        steer_kernel,
        out_shape=jax.ShapeDtypeStruct((tensor, 1, steering.shape[0]), f32),
        in_specs=[VMEM, VMEM, VMEM, VMEM],
        out_specs=VMEM,
        compiler_params=PARAMS,
        name="steer",
    )(sums, w_query, w_kv, token)
    parts = lax.all_to_all(message, "tensor", 0, 0, tiled=True)
    return (query_grad, kv_grad, jnp.sum(parts, axis=(0, 1)))


def solution(mesh):
    placed = (
        P("dp", "tensor"),
        P(None, "dp", "tensor"),
        P("dp", "tensor"),
        P("dp"),
        P("dp", "tensor"),
        P(None, "dp", "tensor"),
        P(None, None, "dp", "tensor"),
        P("dp"),
        P("dp"),
        P(),
    )
    return jax.shard_map(
        shards,
        mesh=mesh,
        in_specs=placed,
        out_specs=(P("dp", "tensor"), P(None, "dp", "tensor"), P("dp")),
        check_vma=False,
    )
```

```python
import functools
import math

import jax
import jax.numpy as jnp
from jax import lax
from jax.experimental import pallas as pl
from jax.experimental.pallas import tpu as pltpu
from jax.sharding import PartitionSpec as P

HD = 128
ROWS = 32
TILE = 256
MASKED = -1e30
NN = (((1,), (0,)), ((), ()))
NT = (((1,), (1,)), ((), ()))
TN = (((0,), (0,)), ((), ()))
VMEM = pl.BlockSpec(memory_space=pltpu.VMEM)
HBM = pl.BlockSpec(memory_space=pltpu.HBM)
SMEM = pl.BlockSpec(memory_space=pltpu.SMEM)
PARAMS = pltpu.CompilerParams(vmem_limit_bytes=40 * 2**20)


def dot(a, b, dims):
    return lax.dot_general(a, b, dims, preferred_element_type=jnp.float32)


def in_thirds(row):
    first = row.astype(jnp.bfloat16).astype(jnp.float32)
    second = (row - first).astype(jnp.bfloat16).astype(jnp.float32)
    third = row - first - second
    rest = jnp.zeros((13, row.shape[1]), jnp.float32)
    return jnp.concatenate([first, second, third, rest], axis=0).astype(jnp.bfloat16)


def in_halves(chunks):
    half = len(chunks) // 2
    rows = [jnp.concatenate(chunks[:half], axis=1), jnp.concatenate(chunks[half:], axis=1)]
    return jnp.concatenate(rows, axis=0)


def summed(blocks):
    total = blocks[0].astype(jnp.float32)
    for peer in range(1, blocks.shape[0]):
        total = total + blocks[peer].astype(jnp.float32)
    return total


def chunk_of(halves, chunk, count):
    row, at = divmod(chunk, count // 2)
    return halves[row : row + 1, at * HD : (at + 1) * HD]


def project_kernel(prompt_id, steering, w_query, w_kv, message, vector, wq, wkv, sems):
    copies = [
        pltpu.make_async_copy(source, held, sems.at[at])
        for at, (source, held) in enumerate(((w_query, wq), (steering, vector), (w_kv, wkv)))
    ]
    for copy in copies:
        copy.start()
    mark = jnp.full((1, HD), prompt_id[0], jnp.int32)
    for copy in copies:
        copy.wait()
    thirds = in_thirds(vector[...])
    parts = [jnp.sum(dot(thirds, w[...], NN), 0, keepdims=True) for w in (wq, wkv.at[0], wkv.at[1])]
    row = jnp.concatenate(parts, axis=1)
    peak = jnp.max(jnp.abs(row), 1, keepdims=True)
    power = jnp.clip(jnp.floor(14.9 - jnp.log2(peak)), -60.0, 60.0)
    whole = jnp.floor(row * jnp.exp2(power) + 0.5).astype(jnp.int32)
    scale = jnp.broadcast_to(power, (1, HD)).astype(jnp.int32)
    chunks = [whole[:, at : at + HD] for at in range(0, whole.shape[1], HD)]
    half = len(chunks) // 2
    block = in_halves(chunks[:half] + [mark] + chunks[half:] + [scale]).astype(jnp.int16)
    for peer in range(message.shape[0]):
        message[peer] = block


def shifts_from(shares):
    last = shares.shape[2] - HD
    total = jnp.zeros((2, last), jnp.float32)
    for peer in range(shares.shape[0]):
        block = shares[peer].astype(jnp.int32).astype(jnp.float32)
        scale = jnp.exp2(-block[1:, last:])
        total = total + block[:, :last] * jnp.concatenate([scale] * (last // HD), axis=1)
    return total


def pick_kernel(shares, cache, outgoing, marks, ids, sems):
    peers = shares.shape[0]
    last = shares.shape[2] - HD
    lane = lax.broadcasted_iota(jnp.int32, (2, HD), 1)
    found = jnp.zeros((2, HD), jnp.int32)
    for peer in range(peers):
        found = jnp.where(lane == peer, shares[peer, :, last:].astype(jnp.int32), found)
    marks[...] = found[:1]
    copy = pltpu.make_async_copy(marks, ids, sems.at[0])
    copy.start()
    copy.wait()
    for peer in range(peers):
        pltpu.make_async_copy(cache.at[:, ids[0, peer]], outgoing.at[peer], sems.at[1]).start()
    pltpu.make_async_copy(outgoing, outgoing, sems.at[1]).wait()


def two_parts(query):
    scaled = query.astype(jnp.float32) * (math.log2(math.e) / math.sqrt(HD))
    high = scaled.astype(jnp.bfloat16)
    lane = lax.broadcasted_iota(jnp.int32, query.shape, 1)
    low = jnp.where(lane == HD - 1, 1.0, scaled - high.astype(jnp.float32)).astype(jnp.bfloat16)
    return jnp.concatenate([high, low], axis=1)


def column(block, at):
    lane = lax.broadcasted_iota(jnp.int32, block.shape, 1)
    return jnp.sum(jnp.where(lane == at, block, 0.0), 1, keepdims=True)


def fill_own(live, keys, keys_two, causal):
    lane = lax.broadcasted_iota(jnp.int32, keys.shape, 1)
    keys_two[:, :HD] = keys
    keys_two[:, HD:] = jnp.where(lane == HD - 1, 0.0, keys.astype(jnp.float32)).astype(jnp.bfloat16)
    token_at = lax.broadcasted_iota(jnp.int32, causal.shape, 0)
    key_at = lax.broadcasted_iota(jnp.int32, causal.shape, 1)
    causal[...] = jnp.where((key_at <= token_at) & (key_at < live), 0.0, MASKED)


def shift_kernel(lens, shares, q_ref, kv_ref, cot_ref, outgoing, queries, outs, own):
    del outgoing
    f32, bf16 = jnp.float32, jnp.bfloat16
    heads = q_ref.shape[1] // HD
    total = shifts_from(shares)
    shift = [chunk_of(total, chunk, heads + 2) for chunk in range(heads + 2)]
    for c in range(2):
        own[c] = (kv_ref[c].astype(f32) + shift[heads + c]).astype(bf16)
    token = lax.broadcasted_iota(jnp.int32, (q_ref.shape[0], HD), 0)
    for head in range(heads):
        columns = slice(head * HD, (head + 1) * HD)
        queries[:, columns] = (q_ref[:, columns].astype(f32) + shift[head]).astype(bf16)
        grad = jnp.where(token < lens[0], cot_ref[:, columns].astype(f32), 0.0)
        outs[:, columns] = grad.astype(bf16)


def prepare_kernel(
    ids, prompt_lens, lens, queries, outs, own, stats, sloped, plain, keys_two, causal
):
    f32, bf16 = jnp.float32, jnp.bfloat16
    heads = queries.shape[1] // HD
    fill_own(lens[0], own[0], keys_two, causal)
    prompt_live = jnp.full((queries.shape[0], 1), prompt_lens[ids[0]], jnp.int32)
    stats[:, 3 * heads : 3 * heads + 1] = prompt_live.astype(f32)
    for head in range(heads):
        columns = slice(head * HD, (head + 1) * HD)
        score = dot(two_parts(queries[:, columns]), keys_two[...], NT) + causal[...]
        top = jnp.max(score, 1, keepdims=True)
        prob = jnp.exp2(score - top)
        slope = prob * dot(outs[:, columns], own[1], NT)
        stats[:, head : head + 1] = top
        stats[:, heads + head : heads + head + 1] = jnp.sum(prob, 1, keepdims=True)
        stats[:, 2 * heads + head : 2 * heads + head + 1] = jnp.sum(slope, 1, keepdims=True)
        sloped[head] = dot(slope.astype(bf16), own[0], NN).astype(bf16)
        plain[head] = dot(prob.astype(bf16), own[0], NN).astype(bf16)


def attend_kernel(
    arrived,
    queries,
    outs,
    stats,
    sloped,
    plain,
    dq_ref,
    message,
    final,
    keys,
    keys_t,
    values_t,
    scores0,
    scores1,
    slopes0,
    slopes1,
    grads0,
    grads1,
    factors0,
    factors1,
    terms0,
    terms1,
):
    f32, bf16 = jnp.float32, jnp.bfloat16
    span = arrived.shape[0] * arrived.shape[2]
    tokens = queries.shape[0]
    heads = queries.shape[1] // HD
    scale = 1.0 / math.sqrt(HD)
    keys[...] = arrived[:, 0].reshape(span, HD)
    keys_t[:HD] = arrived[:, 0].reshape(span, HD).T
    values_t[...] = arrived[:, 1].reshape(span, HD).T
    feature = lax.broadcasted_iota(jnp.int32, (HD, span), 0)
    prompt_live = jnp.broadcast_to(column(stats[:8], 3 * heads), (8, HD))[:1]
    prompt_live = jnp.concatenate([prompt_live] * (span // HD), axis=1)
    place = lax.broadcasted_iota(jnp.int32, (1, span), 1).astype(f32)
    barred = jnp.where(place >= prompt_live, MASKED, 0.0)
    keys_t[HD:] = jnp.where(feature == HD - 1, barred, keys_t[:HD].astype(f32)).astype(bf16)
    scores, slopes = (scores0, scores1), (slopes0, slopes1)
    grads, factors, terms = (grads0, grads1), (factors0, factors1), (terms0, terms1)
    query_sums, key_sums, value_sums = [], [], []
    tiles = span // TILE

    def columns(head):
        return slice(head * HD, (head + 1) * HD)

    def product(head, at, query):
        slot, part = head % 2, slice(at % tiles * TILE, (at % tiles + 1) * TILE)
        if at < tiles:
            scores[slot][:, part] = dot(query, keys_t[:, part], NN)
        else:
            slopes[slot][:, part] = dot(outs[:, columns(head)], values_t[:, part], NN)

    def softmax(head, at):
        slot, rows = head % 2, slice(at * ROWS, (at + 1) * ROWS)
        own_top, own_mass, own_slope = (column(stats[rows], n * heads + head) for n in range(3))
        score = scores[slot][rows]
        top = jnp.maximum(jnp.max(score, 1, keepdims=True), own_top)
        prob = jnp.exp2(score - top)
        share = jnp.exp2(own_top - top)
        slope = slopes[slot][rows]
        inverse = 1.0 / (jnp.sum(prob, 1, keepdims=True) + own_mass * share)
        delta = (jnp.sum(prob * slope, 1, keepdims=True) + own_slope * share) * inverse
        grads[slot][rows] = (prob * (slope - delta)).astype(bf16)
        factor = inverse * scale
        factors[slot][rows] = jnp.broadcast_to(factor, (ROWS, HD))
        own_factor = factor * share
        term = sloped[head, rows].astype(f32) - delta * plain[head, rows].astype(f32)
        terms[slot][rows] = term * own_factor
        by_query = (own_slope - delta * own_mass) * own_factor
        by_out = own_mass * share * inverse
        key_sums.append(by_query * queries[rows, columns(head)].astype(f32))
        value_sums.append(by_out * outs[rows, columns(head)].astype(f32))
        for n, value in enumerate((top, inverse, delta)):
            final[rows, n * heads + head : n * heads + head + 1] = value

    def gradient(head, at, total):
        slot = head % 2
        if at < tiles:
            part = slice(at * TILE, (at + 1) * TILE)
            term = dot(grads[slot][:, part], keys[part], NN)
            return term if total is None else total + term
        total = total * factors[slot][...] + terms[slot][...]
        dq_ref[:, columns(head)] = total.astype(bf16)
        query_sums.append(jnp.sum(total, 0, keepdims=True))
        return total

    query = two_parts(queries[:, columns(0)])
    for at in range(2 * tiles):
        product(0, at, query)
    chunks = tokens // ROWS
    for head in range(heads):
        if head + 1 < heads:
            query = two_parts(queries[:, columns(head + 1)])
        total, done, made = None, 0, 0
        for chunk in range(chunks):
            while head + 1 < heads and made < 2 * tiles * (chunk + 1) // chunks:
                product(head + 1, made, query)
                made += 1
            while head > 0 and done < (tiles + 1) * (chunk + 1) // chunks:
                total = gradient(head - 1, done, total)
                done += 1
            softmax(head, chunk)
    total = None
    for at in range(tiles + 1):
        total = gradient(heads - 1, at, total)
    last = [jnp.sum(sum(rows), 0, keepdims=True) for rows in (key_sums, value_sums)]
    block = in_halves(query_sums + last).astype(bf16)
    for peer in range(message.shape[0]):
        message[peer] = block


def finish_kernel(
    lens, queries, outs, own, final, dq, dq_out, dkv_ref, token, keys_two, causal, sem
):
    bf16 = jnp.bfloat16
    copy = pltpu.make_async_copy(dq, dq_out, sem)
    copy.start()
    heads = queries.shape[1] // HD
    fill_own(lens[0], own[0], keys_two, causal)
    grad_keys = grad_values = None
    for head in range(heads):
        columns = slice(head * HD, (head + 1) * HD)
        top, inverse, delta = (column(final[...], n * heads + head) for n in range(3))
        query, grad = queries[:, columns], outs[:, columns]
        score = dot(two_parts(query), keys_two[...], NT) + causal[...]
        prob = jnp.exp2(score - top) * inverse
        mine = (prob * (dot(grad, own[1], NT) - delta) * (1.0 / math.sqrt(HD))).astype(bf16)
        by_key = dot(mine, query, TN)
        by_value = dot(prob.astype(bf16), grad, TN)
        grad_keys = by_key if head == 0 else grad_keys + by_key
        grad_values = by_value if head == 0 else grad_values + by_value
    dkv_ref[0] = grad_keys.astype(bf16)
    dkv_ref[1] = grad_values.astype(bf16)
    token[...] = jnp.zeros_like(token)
    copy.wait()


def steer_kernel(sums, w_query, w_kv, token, message):
    del token
    total = summed(sums)
    heads = w_query.shape[1] // HD
    chunks = [chunk_of(total, chunk, heads + 2) for chunk in range(heads + 2)]
    part = dot(in_thirds(jnp.concatenate(chunks[:heads], axis=1)), w_query[...], NT)
    for c in range(2):
        part = part + dot(in_thirds(chunks[heads + c]), w_kv[c], NT)
    row = jnp.sum(part, 0, keepdims=True)
    for peer in range(message.shape[0]):
        message[peer] = row


def shards(
    q_base,
    kv_base,
    cotangent,
    steering,
    w_query,
    w_kv,
    prompt_cache,
    prompt_ids,
    dialogue_lens,
    prompt_lens,
):
    dp = lax.axis_size("dp")
    tensor = lax.axis_size("tensor")
    f32 = jnp.float32
    tokens, width = q_base.shape
    positions = prompt_cache.shape[2]
    half_width = (width + 2 * HD) // 2
    bf16 = jnp.bfloat16
    message = pl.pallas_call(
        project_kernel,
        out_shape=jax.ShapeDtypeStruct((dp, 2, half_width + HD), jnp.int16),
        in_specs=[SMEM, HBM, HBM, HBM],
        out_specs=VMEM,
        scratch_shapes=[
            pltpu.VMEM((1, steering.shape[0]), f32),
            pltpu.VMEM(w_query.shape, bf16),
            pltpu.VMEM(w_kv.shape, bf16),
            pltpu.SemaphoreType.DMA((3,)),
        ],
        compiler_params=pltpu.CompilerParams(vmem_limit_bytes=63 * 2**20),
        name="project",
    )(prompt_ids, steering.reshape(1, -1), w_query, w_kv)
    shares = lax.all_to_all(message, "dp", 0, 0, tiled=True)
    outgoing = pl.pallas_call(
        pick_kernel,
        out_shape=jax.ShapeDtypeStruct((dp, 2, positions, HD), bf16),
        in_specs=[VMEM, VMEM],
        out_specs=HBM,
        scratch_shapes=[
            pltpu.VMEM((1, HD), jnp.int32),
            pltpu.SMEM((1, HD), jnp.int32),
            pltpu.SemaphoreType.DMA((2,)),
        ],
        compiler_params=PARAMS,
        name="pick",
    )(shares, prompt_cache)
    arrived = lax.all_to_all(outgoing, "dp", 0, 0, tiled=True)
    heads = width // HD
    span = dp * positions
    by_head = jax.ShapeDtypeStruct((heads, tokens, HD), bf16)
    by_row = jax.ShapeDtypeStruct((tokens, HD), f32)
    own_scratch = [pltpu.VMEM((tokens, 2 * HD), bf16), pltpu.VMEM((tokens, tokens), f32)]
    queries, outs, own = pl.pallas_call(
        shift_kernel,
        out_shape=(
            jax.ShapeDtypeStruct((tokens, width), bf16),
            jax.ShapeDtypeStruct((tokens, width), bf16),
            jax.ShapeDtypeStruct((2, tokens, HD), bf16),
        ),
        in_specs=[SMEM, VMEM, VMEM, VMEM, VMEM, HBM],
        out_specs=(VMEM,) * 3,
        compiler_params=PARAMS,
        name="shift",
    )(dialogue_lens, shares, q_base, kv_base, cotangent, outgoing)
    stats, sloped, plain = pl.pallas_call(
        prepare_kernel,
        out_shape=(by_row, by_head, by_head),
        in_specs=[SMEM, SMEM, SMEM, VMEM, VMEM, VMEM],
        out_specs=(VMEM,) * 3,
        scratch_shapes=own_scratch,
        compiler_params=PARAMS,
        name="prepare",
    )(prompt_ids, prompt_lens, dialogue_lens, queries, outs, own)
    held_grad, message, final = pl.pallas_call(
        attend_kernel,
        out_shape=(
            jax.ShapeDtypeStruct(q_base.shape, bf16),
            jax.ShapeDtypeStruct((dp, 2, half_width), bf16),
            by_row,
        ),
        in_specs=[VMEM] * 6,
        out_specs=(VMEM, VMEM, VMEM),
        scratch_shapes=[
            pltpu.VMEM((span, HD), bf16),
            pltpu.VMEM((2 * HD, span), bf16),
            pltpu.VMEM((HD, span), bf16),
        ]
        + [
            pltpu.VMEM((tokens, columns), kind)
            for columns, kind in ((span, f32), (span, f32), (span, bf16), (HD, f32), (HD, f32))
            for slot in range(2)
        ],
        compiler_params=PARAMS,
        name="attend",
    )(arrived, queries, outs, stats, sloped, plain)
    query_grad, kv_grad, token = pl.pallas_call(
        finish_kernel,
        out_shape=(
            jax.ShapeDtypeStruct(q_base.shape, bf16),
            jax.ShapeDtypeStruct(kv_base.shape, bf16),
            jax.ShapeDtypeStruct((8, HD), f32),
        ),
        in_specs=[SMEM] + [VMEM] * 5,
        out_specs=(HBM, VMEM, VMEM),
        scratch_shapes=own_scratch + [pltpu.SemaphoreType.DMA],
        compiler_params=PARAMS,
        name="finish",
    )(dialogue_lens, queries, outs, own, final, held_grad)
    sums = lax.all_to_all(message, "dp", 0, 0, tiled=True)
    message = pl.pallas_call(
        steer_kernel,
        out_shape=jax.ShapeDtypeStruct((tensor, 1, steering.shape[0]), f32),
        in_specs=[VMEM, VMEM, VMEM, VMEM],
        out_specs=VMEM,
        compiler_params=PARAMS,
        name="steer",
    )(sums, w_query, w_kv, token)
    parts = lax.all_to_all(message, "tensor", 0, 0, tiled=True)
    return (query_grad, kv_grad, jnp.sum(parts, axis=(0, 1)))


def solution(mesh):
    placed = (
        P("dp", "tensor"),
        P(None, "dp", "tensor"),
        P("dp", "tensor"),
        P("dp"),
        P("dp", "tensor"),
        P(None, "dp", "tensor"),
        P(None, None, "dp", "tensor"),
        P("dp"),
        P("dp"),
        P(),
    )
    return jax.shard_map(
        shards,
        mesh=mesh,
        in_specs=placed,
        out_specs=(P("dp", "tensor"), P(None, "dp", "tensor"), P("dp")),
        check_vma=False,
    )
```

```python
import functools
import math

import jax
import jax.numpy as jnp
from jax import lax
from jax.experimental import pallas as pl
from jax.experimental.pallas import tpu as pltpu
from jax.sharding import PartitionSpec as P

HD = 128
ROWS = 32
TILE = 256
MASKED = -1e30
NN = (((1,), (0,)), ((), ()))
NT = (((1,), (1,)), ((), ()))
TN = (((0,), (0,)), ((), ()))
VMEM = pl.BlockSpec(memory_space=pltpu.VMEM)
HBM = pl.BlockSpec(memory_space=pltpu.HBM)
SMEM = pl.BlockSpec(memory_space=pltpu.SMEM)
PARAMS = pltpu.CompilerParams(vmem_limit_bytes=40 * 2**20)


def dot(a, b, dims):
    return lax.dot_general(a, b, dims, preferred_element_type=jnp.float32)


def in_thirds(row):
    first = row.astype(jnp.bfloat16).astype(jnp.float32)
    second = (row - first).astype(jnp.bfloat16).astype(jnp.float32)
    third = row - first - second
    rest = jnp.zeros((13, row.shape[1]), jnp.float32)
    return jnp.concatenate([first, second, third, rest], axis=0).astype(jnp.bfloat16)


def in_halves(chunks):
    half = len(chunks) // 2
    rows = [jnp.concatenate(chunks[:half], axis=1), jnp.concatenate(chunks[half:], axis=1)]
    return jnp.concatenate(rows, axis=0)


def summed(blocks):
    total = blocks[0].astype(jnp.float32)
    for peer in range(1, blocks.shape[0]):
        total = total + blocks[peer].astype(jnp.float32)
    return total


def chunk_of(halves, chunk, count):
    row, at = divmod(chunk, count // 2)
    return halves[row : row + 1, at * HD : (at + 1) * HD]


def project_kernel(prompt_id, steering, w_query, w_kv, message, vector, wq, wkv, sems):
    copies = [
        pltpu.make_async_copy(source, held, sems.at[at])
        for at, (source, held) in enumerate(((w_query, wq), (steering, vector), (w_kv, wkv)))
    ]
    for copy in copies:
        copy.start()
    mark = jnp.full((1, HD), prompt_id[0], jnp.int32)
    for copy in copies:
        copy.wait()
    thirds = in_thirds(vector[...])
    parts = [jnp.sum(dot(thirds, w[...], NN), 0, keepdims=True) for w in (wq, wkv.at[0], wkv.at[1])]
    row = jnp.concatenate(parts, axis=1)
    peak = jnp.max(jnp.abs(row), 1, keepdims=True)
    power = jnp.clip(jnp.floor(14.9 - jnp.log2(peak)), -60.0, 60.0)
    whole = jnp.floor(row * jnp.exp2(power) + 0.5).astype(jnp.int32)
    scale = jnp.broadcast_to(power, (1, HD)).astype(jnp.int32)
    chunks = [whole[:, at : at + HD] for at in range(0, whole.shape[1], HD)]
    half = len(chunks) // 2
    block = in_halves(chunks[:half] + [mark] + chunks[half:] + [scale]).astype(jnp.int16)
    for peer in range(message.shape[0]):
        message[peer] = block


def shifts_from(shares):
    last = shares.shape[2] - HD
    total = jnp.zeros((2, last), jnp.float32)
    for peer in range(shares.shape[0]):
        block = shares[peer].astype(jnp.int32).astype(jnp.float32)
        scale = jnp.exp2(-block[1:, last:])
        total = total + block[:, :last] * jnp.concatenate([scale] * (last // HD), axis=1)
    return total


def pick_kernel(shares, cache, outgoing, marks, ids, sems):
    peers = shares.shape[0]
    last = shares.shape[2] - HD
    lane = lax.broadcasted_iota(jnp.int32, (2, HD), 1)
    found = jnp.zeros((2, HD), jnp.int32)
    for peer in range(peers):
        found = jnp.where(lane == peer, shares[peer, :, last:].astype(jnp.int32), found)
    marks[...] = found[:1]
    copy = pltpu.make_async_copy(marks, ids, sems.at[0])
    copy.start()
    copy.wait()
    for peer in range(peers):
        pltpu.make_async_copy(cache.at[:, ids[0, peer]], outgoing.at[peer], sems.at[1]).start()
    pltpu.make_async_copy(outgoing, outgoing, sems.at[1]).wait()


def two_parts(query):
    scaled = query.astype(jnp.float32) * (math.log2(math.e) / math.sqrt(HD))
    high = scaled.astype(jnp.bfloat16)
    lane = lax.broadcasted_iota(jnp.int32, query.shape, 1)
    low = jnp.where(lane == HD - 1, 1.0, scaled - high.astype(jnp.float32)).astype(jnp.bfloat16)
    return jnp.concatenate([high, low], axis=1)


def column(block, at):
    lane = lax.broadcasted_iota(jnp.int32, block.shape, 1)
    return jnp.sum(jnp.where(lane == at, block, 0.0), 1, keepdims=True)


def fill_own(live, keys, keys_two, causal):
    lane = lax.broadcasted_iota(jnp.int32, keys.shape, 1)
    keys_two[:, :HD] = keys
    keys_two[:, HD:] = jnp.where(lane == HD - 1, 0.0, keys.astype(jnp.float32)).astype(jnp.bfloat16)
    token_at = lax.broadcasted_iota(jnp.int32, causal.shape, 0)
    key_at = lax.broadcasted_iota(jnp.int32, causal.shape, 1)
    causal[...] = jnp.where((key_at <= token_at) & (key_at < live), 0.0, MASKED)


def shift_kernel(lens, shares, q_ref, kv_ref, cot_ref, outgoing, queries, outs, own):
    del outgoing
    f32, bf16 = jnp.float32, jnp.bfloat16
    heads = q_ref.shape[1] // HD
    total = shifts_from(shares)
    shift = [chunk_of(total, chunk, heads + 2) for chunk in range(heads + 2)]
    for c in range(2):
        own[c] = (kv_ref[c].astype(f32) + shift[heads + c]).astype(bf16)
    token = lax.broadcasted_iota(jnp.int32, (q_ref.shape[0], HD), 0)
    for head in range(heads):
        columns = slice(head * HD, (head + 1) * HD)
        queries[:, columns] = (q_ref[:, columns].astype(f32) + shift[head]).astype(bf16)
        grad = jnp.where(token < lens[0], cot_ref[:, columns].astype(f32), 0.0)
        outs[:, columns] = grad.astype(bf16)


def prepare_kernel(
    ids, prompt_lens, lens, queries, outs, own, stats, sloped, plain, keys_two, causal
):
    f32, bf16 = jnp.float32, jnp.bfloat16
    heads = queries.shape[1] // HD
    fill_own(lens[0], own[0], keys_two, causal)
    prompt_live = jnp.full((queries.shape[0], 1), prompt_lens[ids[0]], jnp.int32)
    stats[:, 2 * heads : 2 * heads + 1] = prompt_live.astype(f32)
    for head in range(heads):
        columns = slice(head * HD, (head + 1) * HD)
        score = dot(two_parts(queries[:, columns]), keys_two[...], NT) + causal[...]
        top = jnp.max(score, 1, keepdims=True)
        prob = jnp.exp2(score - top)
        mass = jnp.sum(prob, 1, keepdims=True)
        prob = prob * (1.0 / mass)
        slope = dot(outs[:, columns], own[1], NT)
        delta = jnp.sum(prob * slope, 1, keepdims=True)
        slope = prob * (slope - delta)
        stats[:, head : head + 1] = top + jnp.log2(mass)
        stats[:, heads + head : heads + head + 1] = delta
        sloped[head] = dot(slope.astype(bf16), own[0], NN).astype(bf16)
        plain[head] = dot(prob.astype(bf16), own[0], NN).astype(bf16)


def attend_kernel(
    arrived,
    queries,
    outs,
    stats,
    sloped,
    plain,
    dq_ref,
    message,
    final,
    keys,
    keys_t,
    values_t,
    scores0,
    scores1,
    slopes0,
    slopes1,
    grads0,
    grads1,
    factors0,
    factors1,
    terms0,
    terms1,
):
    f32, bf16 = jnp.float32, jnp.bfloat16
    span = arrived.shape[0] * arrived.shape[2]
    tokens = queries.shape[0]
    heads = queries.shape[1] // HD
    scale = 1.0 / math.sqrt(HD)
    keys[...] = arrived[:, 0].reshape(span, HD)
    keys_t[:HD] = arrived[:, 0].reshape(span, HD).T
    values_t[...] = arrived[:, 1].reshape(span, HD).T
    feature = lax.broadcasted_iota(jnp.int32, (HD, span), 0)
    prompt_live = jnp.broadcast_to(column(stats[:8], 2 * heads), (8, HD))[:1]
    prompt_live = jnp.concatenate([prompt_live] * (span // HD), axis=1)
    place = lax.broadcasted_iota(jnp.int32, (1, span), 1).astype(f32)
    barred = jnp.where(place >= prompt_live, MASKED, 0.0)
    keys_t[HD:] = jnp.where(feature == HD - 1, barred, keys_t[:HD].astype(f32)).astype(bf16)
    scores, slopes = (scores0, scores1), (slopes0, slopes1)
    grads, factors, terms = (grads0, grads1), (factors0, factors1), (terms0, terms1)
    query_sums, key_sums, value_sums = [], [], []
    tiles = span // TILE

    def columns(head):
        return slice(head * HD, (head + 1) * HD)

    def product(head, at, query):
        slot, part = head % 2, slice(at % tiles * TILE, (at % tiles + 1) * TILE)
        if at < tiles:
            scores[slot][:, part] = dot(query, keys_t[:, part], NN)
        else:
            slopes[slot][:, part] = dot(outs[:, columns(head)], values_t[:, part], NN)

    def softmax(head, at):
        slot, rows = head % 2, slice(at * ROWS, (at + 1) * ROWS)
        own_top, own_delta = (column(stats[rows], n * heads + head) for n in range(2))
        score = scores[slot][rows]
        top = jnp.maximum(jnp.max(score, 1, keepdims=True), own_top)
        prob = jnp.exp2(score - top)
        share = jnp.exp2(own_top - top)
        slope = slopes[slot][rows]
        inverse = 1.0 / (jnp.sum(prob, 1, keepdims=True) + share)
        delta = (jnp.sum(prob * slope, 1, keepdims=True) + own_delta * share) * inverse
        grads[slot][rows] = (prob * (slope - delta)).astype(bf16)
        factor = inverse * scale
        factors[slot][rows] = jnp.broadcast_to(factor, (ROWS, HD))
        own_factor = factor * share
        apart = own_delta - delta
        term = sloped[head, rows].astype(f32) + apart * plain[head, rows].astype(f32)
        terms[slot][rows] = term * own_factor
        by_query = apart * own_factor
        by_out = share * inverse
        key_sums.append(by_query * queries[rows, columns(head)].astype(f32))
        value_sums.append(by_out * outs[rows, columns(head)].astype(f32))
        for n, value in enumerate((top, inverse, delta)):
            final[rows, n * heads + head : n * heads + head + 1] = value

    def gradient(head, at, total):
        slot = head % 2
        if at < tiles:
            part = slice(at * TILE, (at + 1) * TILE)
            term = dot(grads[slot][:, part], keys[part], NN)
            return term if total is None else total + term
        total = total * factors[slot][...] + terms[slot][...]
        dq_ref[:, columns(head)] = total.astype(bf16)
        query_sums.append(jnp.sum(total, 0, keepdims=True))
        return total

    query = two_parts(queries[:, columns(0)])
    for at in range(2 * tiles):
        product(0, at, query)
    chunks = tokens // ROWS
    for head in range(heads):
        if head + 1 < heads:
            query = two_parts(queries[:, columns(head + 1)])
        total, done, made = None, 0, 0
        for chunk in range(chunks):
            while head + 1 < heads and made < 2 * tiles * (chunk + 1) // chunks:
                product(head + 1, made, query)
                made += 1
            while head > 0 and done < (tiles + 1) * (chunk + 1) // chunks:
                total = gradient(head - 1, done, total)
                done += 1
            softmax(head, chunk)
    total = None
    for at in range(tiles + 1):
        total = gradient(heads - 1, at, total)
    last = [jnp.sum(sum(rows), 0, keepdims=True) for rows in (key_sums, value_sums)]
    block = in_halves(query_sums + last).astype(bf16)
    for peer in range(message.shape[0]):
        message[peer] = block


def finish_kernel(
    lens, queries, outs, own, final, dq, dq_out, dkv_ref, token, keys_two, causal, sem
):
    bf16 = jnp.bfloat16
    copy = pltpu.make_async_copy(dq, dq_out, sem)
    copy.start()
    heads = queries.shape[1] // HD
    fill_own(lens[0], own[0], keys_two, causal)
    grad_keys = grad_values = None
    for head in range(heads):
        columns = slice(head * HD, (head + 1) * HD)
        top, inverse, delta = (column(final[...], n * heads + head) for n in range(3))
        query, grad = queries[:, columns], outs[:, columns]
        score = dot(two_parts(query), keys_two[...], NT) + causal[...]
        prob = jnp.exp2(score - top) * inverse
        mine = (prob * (dot(grad, own[1], NT) - delta) * (1.0 / math.sqrt(HD))).astype(bf16)
        by_key = dot(mine, query, TN)
        by_value = dot(prob.astype(bf16), grad, TN)
        grad_keys = by_key if head == 0 else grad_keys + by_key
        grad_values = by_value if head == 0 else grad_values + by_value
    dkv_ref[0] = grad_keys.astype(bf16)
    dkv_ref[1] = grad_values.astype(bf16)
    token[...] = jnp.zeros_like(token)
    copy.wait()


def steer_kernel(sums, w_query, w_kv, token, message):
    del token
    total = summed(sums)
    heads = w_query.shape[1] // HD
    chunks = [chunk_of(total, chunk, heads + 2) for chunk in range(heads + 2)]
    part = dot(in_thirds(jnp.concatenate(chunks[:heads], axis=1)), w_query[...], NT)
    for c in range(2):
        part = part + dot(in_thirds(chunks[heads + c]), w_kv[c], NT)
    row = jnp.sum(part, 0, keepdims=True)
    for peer in range(message.shape[0]):
        message[peer] = row


def shards(
    q_base,
    kv_base,
    cotangent,
    steering,
    w_query,
    w_kv,
    prompt_cache,
    prompt_ids,
    dialogue_lens,
    prompt_lens,
):
    dp = lax.axis_size("dp")
    tensor = lax.axis_size("tensor")
    f32 = jnp.float32
    tokens, width = q_base.shape
    positions = prompt_cache.shape[2]
    half_width = (width + 2 * HD) // 2
    bf16 = jnp.bfloat16
    message = pl.pallas_call(
        project_kernel,
        out_shape=jax.ShapeDtypeStruct((dp, 2, half_width + HD), jnp.int16),
        in_specs=[SMEM, HBM, HBM, HBM],
        out_specs=VMEM,
        scratch_shapes=[
            pltpu.VMEM((1, steering.shape[0]), f32),
            pltpu.VMEM(w_query.shape, bf16),
            pltpu.VMEM(w_kv.shape, bf16),
            pltpu.SemaphoreType.DMA((3,)),
        ],
        compiler_params=pltpu.CompilerParams(vmem_limit_bytes=63 * 2**20),
        name="project",
    )(prompt_ids, steering.reshape(1, -1), w_query, w_kv)
    shares = lax.all_to_all(message, "dp", 0, 0, tiled=True)
    outgoing = pl.pallas_call(
        pick_kernel,
        out_shape=jax.ShapeDtypeStruct((dp, 2, positions, HD), bf16),
        in_specs=[VMEM, VMEM],
        out_specs=HBM,
        scratch_shapes=[
            pltpu.VMEM((1, HD), jnp.int32),
            pltpu.SMEM((1, HD), jnp.int32),
            pltpu.SemaphoreType.DMA((2,)),
        ],
        compiler_params=PARAMS,
        name="pick",
    )(shares, prompt_cache)
    arrived = lax.all_to_all(outgoing, "dp", 0, 0, tiled=True)
    heads = width // HD
    span = dp * positions
    by_head = jax.ShapeDtypeStruct((heads, tokens, HD), bf16)
    by_row = jax.ShapeDtypeStruct((tokens, HD), f32)
    own_scratch = [pltpu.VMEM((tokens, 2 * HD), bf16), pltpu.VMEM((tokens, tokens), f32)]
    queries, outs, own = pl.pallas_call(
        shift_kernel,
        out_shape=(
            jax.ShapeDtypeStruct((tokens, width), bf16),
            jax.ShapeDtypeStruct((tokens, width), bf16),
            jax.ShapeDtypeStruct((2, tokens, HD), bf16),
        ),
        in_specs=[SMEM, VMEM, VMEM, VMEM, VMEM, HBM],
        out_specs=(VMEM,) * 3,
        compiler_params=PARAMS,
        name="shift",
    )(dialogue_lens, shares, q_base, kv_base, cotangent, outgoing)
    stats, sloped, plain = pl.pallas_call(
        prepare_kernel,
        out_shape=(by_row, by_head, by_head),
        in_specs=[SMEM, SMEM, SMEM, VMEM, VMEM, VMEM],
        out_specs=(VMEM,) * 3,
        scratch_shapes=own_scratch,
        compiler_params=PARAMS,
        name="prepare",
    )(prompt_ids, prompt_lens, dialogue_lens, queries, outs, own)
    held_grad, message, final = pl.pallas_call(
        attend_kernel,
        out_shape=(
            jax.ShapeDtypeStruct(q_base.shape, bf16),
            jax.ShapeDtypeStruct((dp, 2, half_width), bf16),
            by_row,
        ),
        in_specs=[VMEM] * 6,
        out_specs=(VMEM, VMEM, VMEM),
        scratch_shapes=[
            pltpu.VMEM((span, HD), bf16),
            pltpu.VMEM((2 * HD, span), bf16),
            pltpu.VMEM((HD, span), bf16),
        ]
        + [
            pltpu.VMEM((tokens, columns), kind)
            for columns, kind in ((span, f32), (span, f32), (span, bf16), (HD, f32), (HD, f32))
            for slot in range(2)
        ],
        compiler_params=PARAMS,
        name="attend",
    )(arrived, queries, outs, stats, sloped, plain)
    query_grad, kv_grad, token = pl.pallas_call(
        finish_kernel,
        out_shape=(
            jax.ShapeDtypeStruct(q_base.shape, bf16),
            jax.ShapeDtypeStruct(kv_base.shape, bf16),
            jax.ShapeDtypeStruct((8, HD), f32),
        ),
        in_specs=[SMEM] + [VMEM] * 5,
        out_specs=(HBM, VMEM, VMEM),
        scratch_shapes=own_scratch + [pltpu.SemaphoreType.DMA],
        compiler_params=PARAMS,
        name="finish",
    )(dialogue_lens, queries, outs, own, final, held_grad)
    sums = lax.all_to_all(message, "dp", 0, 0, tiled=True)
    message = pl.pallas_call(
        steer_kernel,
        out_shape=jax.ShapeDtypeStruct((tensor, 1, steering.shape[0]), f32),
        in_specs=[VMEM, VMEM, VMEM, VMEM],
        out_specs=VMEM,
        compiler_params=PARAMS,
        name="steer",
    )(sums, w_query, w_kv, token)
    parts = lax.all_to_all(message, "tensor", 0, 0, tiled=True)
    return (query_grad, kv_grad, jnp.sum(parts, axis=(0, 1)))


def solution(mesh):
    placed = (
        P("dp", "tensor"),
        P(None, "dp", "tensor"),
        P("dp", "tensor"),
        P("dp"),
        P("dp", "tensor"),
        P(None, "dp", "tensor"),
        P(None, None, "dp", "tensor"),
        P("dp"),
        P("dp"),
        P(),
    )
    return jax.shard_map(
        shards,
        mesh=mesh,
        in_specs=placed,
        out_specs=(P("dp", "tensor"), P(None, "dp", "tensor"), P("dp")),
        check_vma=False,
    )
```

```python
import functools
import math

import jax
import jax.numpy as jnp
from jax import lax
from jax.experimental import pallas as pl
from jax.experimental.pallas import tpu as pltpu
from jax.sharding import PartitionSpec as P

HD = 128
ROWS = 32
TILE = 256
MASKED = -1e30
NN = (((1,), (0,)), ((), ()))
NT = (((1,), (1,)), ((), ()))
TN = (((0,), (0,)), ((), ()))
VMEM = pl.BlockSpec(memory_space=pltpu.VMEM)
HBM = pl.BlockSpec(memory_space=pltpu.HBM)
SMEM = pl.BlockSpec(memory_space=pltpu.SMEM)
PARAMS = pltpu.CompilerParams(vmem_limit_bytes=40 * 2**20)


def dot(a, b, dims):
    return lax.dot_general(a, b, dims, preferred_element_type=jnp.float32)


def in_thirds(row):
    first = row.astype(jnp.bfloat16).astype(jnp.float32)
    second = (row - first).astype(jnp.bfloat16).astype(jnp.float32)
    third = row - first - second
    rest = jnp.zeros((13, row.shape[1]), jnp.float32)
    return jnp.concatenate([first, second, third, rest], axis=0).astype(jnp.bfloat16)


def in_halves(chunks):
    half = len(chunks) // 2
    rows = [jnp.concatenate(chunks[:half], axis=1), jnp.concatenate(chunks[half:], axis=1)]
    return jnp.concatenate(rows, axis=0)


def summed(blocks):
    total = blocks[0].astype(jnp.float32)
    for peer in range(1, blocks.shape[0]):
        total = total + blocks[peer].astype(jnp.float32)
    return total


def chunk_of(halves, chunk, count):
    row, at = divmod(chunk, count // 2)
    return halves[row : row + 1, at * HD : (at + 1) * HD]


def project_kernel(prompt_id, steering, w_query, w_kv, message, vector, wq, wkv, sems):
    copies = [
        pltpu.make_async_copy(source, held, sems.at[at])
        for at, (source, held) in enumerate(((w_query, wq), (steering, vector), (w_kv, wkv)))
    ]
    for copy in copies:
        copy.start()
    mark = jnp.full((1, HD), prompt_id[0], jnp.int32)
    for copy in copies:
        copy.wait()
    thirds = in_thirds(vector[...])
    parts = [jnp.sum(dot(thirds, w[...], NN), 0, keepdims=True) for w in (wq, wkv.at[0], wkv.at[1])]
    row = jnp.concatenate(parts, axis=1)
    peak = jnp.max(jnp.abs(row), 1, keepdims=True)
    power = jnp.clip(jnp.floor(14.9 - jnp.log2(peak)), -60.0, 60.0)
    whole = jnp.floor(row * jnp.exp2(power) + 0.5).astype(jnp.int32)
    scale = jnp.broadcast_to(power, (1, HD)).astype(jnp.int32)
    chunks = [whole[:, at : at + HD] for at in range(0, whole.shape[1], HD)]
    half = len(chunks) // 2
    block = in_halves(chunks[:half] + [mark] + chunks[half:] + [scale]).astype(jnp.int16)
    for peer in range(message.shape[0]):
        message[peer] = block


def shifts_from(shares):
    last = shares.shape[2] - HD
    total = jnp.zeros((2, last), jnp.float32)
    for peer in range(shares.shape[0]):
        block = shares[peer].astype(jnp.int32).astype(jnp.float32)
        scale = jnp.exp2(-block[1:, last:])
        total = total + block[:, :last] * jnp.concatenate([scale] * (last // HD), axis=1)
    return total


def pick_kernel(shares, cache, outgoing, marks, ids, sems):
    peers = shares.shape[0]
    last = shares.shape[2] - HD
    lane = lax.broadcasted_iota(jnp.int32, (2, HD), 1)
    half = peers // 2
    fetches = []
    for side in range(2):
        found = jnp.zeros((2, HD), jnp.int32)
        for peer in range(side * half, (side + 1) * half):
            found = jnp.where(lane == peer, shares[peer, :, last:].astype(jnp.int32), found)
        marks[side] = found[:1]
        fetches.append(pltpu.make_async_copy(marks.at[side], ids.at[side], sems.at[2 * side]))
        fetches[side].start()
    for side in range(2):
        fetches[side].wait()
        for peer in range(side * half, (side + 1) * half):
            rows = cache.at[:, ids[side, 0, peer]]
            pltpu.make_async_copy(rows, outgoing.at[peer], sems.at[1]).start()
    pltpu.make_async_copy(outgoing, outgoing, sems.at[1]).wait()


def two_parts(query):
    scaled = query.astype(jnp.float32) * (math.log2(math.e) / math.sqrt(HD))
    high = scaled.astype(jnp.bfloat16)
    lane = lax.broadcasted_iota(jnp.int32, query.shape, 1)
    low = jnp.where(lane == HD - 1, 1.0, scaled - high.astype(jnp.float32)).astype(jnp.bfloat16)
    return jnp.concatenate([high, low], axis=1)


def column(block, at):
    lane = lax.broadcasted_iota(jnp.int32, block.shape, 1)
    return jnp.sum(jnp.where(lane == at, block, 0.0), 1, keepdims=True)


def fill_own(live, keys, keys_two, causal):
    lane = lax.broadcasted_iota(jnp.int32, keys.shape, 1)
    keys_two[:, :HD] = keys
    keys_two[:, HD:] = jnp.where(lane == HD - 1, 0.0, keys.astype(jnp.float32)).astype(jnp.bfloat16)
    token_at = lax.broadcasted_iota(jnp.int32, causal.shape, 0)
    key_at = lax.broadcasted_iota(jnp.int32, causal.shape, 1)
    causal[...] = jnp.where((key_at <= token_at) & (key_at < live), 0.0, MASKED)


def shift_kernel(lens, shares, q_ref, kv_ref, cot_ref, outgoing, queries, outs, own):
    del outgoing
    f32, bf16 = jnp.float32, jnp.bfloat16
    heads = q_ref.shape[1] // HD
    total = shifts_from(shares)
    shift = [chunk_of(total, chunk, heads + 2) for chunk in range(heads + 2)]
    for c in range(2):
        own[c] = (kv_ref[c].astype(f32) + shift[heads + c]).astype(bf16)
    token = lax.broadcasted_iota(jnp.int32, (q_ref.shape[0], HD), 0)
    for head in range(heads):
        columns = slice(head * HD, (head + 1) * HD)
        queries[:, columns] = (q_ref[:, columns].astype(f32) + shift[head]).astype(bf16)
        grad = jnp.where(token < lens[0], cot_ref[:, columns].astype(f32), 0.0)
        outs[:, columns] = grad.astype(bf16)


def prepare_kernel(
    ids, prompt_lens, lens, queries, outs, own, stats, sloped, plain, keys_two, causal
):
    f32, bf16 = jnp.float32, jnp.bfloat16
    heads = queries.shape[1] // HD
    fill_own(lens[0], own[0], keys_two, causal)
    prompt_live = jnp.full((queries.shape[0], 1), prompt_lens[ids[0]], jnp.int32)
    stats[:, 2 * heads : 2 * heads + 1] = prompt_live.astype(f32)
    for head in range(heads):
        columns = slice(head * HD, (head + 1) * HD)
        score = dot(two_parts(queries[:, columns]), keys_two[...], NT) + causal[...]
        top = jnp.max(score, 1, keepdims=True)
        prob = jnp.exp2(score - top)
        mass = jnp.sum(prob, 1, keepdims=True)
        prob = prob * (1.0 / mass)
        slope = dot(outs[:, columns], own[1], NT)
        delta = jnp.sum(prob * slope, 1, keepdims=True)
        slope = prob * (slope - delta)
        stats[:, head : head + 1] = top + jnp.log2(mass)
        stats[:, heads + head : heads + head + 1] = delta
        sloped[head] = dot(slope.astype(bf16), own[0], NN).astype(bf16)
        plain[head] = dot(prob.astype(bf16), own[0], NN).astype(bf16)


def attend_kernel(
    arrived,
    queries,
    outs,
    stats,
    sloped,
    plain,
    dq_ref,
    message,
    final,
    keys,
    keys_t,
    values_t,
    scores0,
    scores1,
    slopes0,
    slopes1,
    grads0,
    grads1,
    factors0,
    factors1,
    terms0,
    terms1,
):
    f32, bf16 = jnp.float32, jnp.bfloat16
    span = arrived.shape[0] * arrived.shape[2]
    tokens = queries.shape[0]
    heads = queries.shape[1] // HD
    scale = 1.0 / math.sqrt(HD)
    keys[...] = arrived[:, 0].reshape(span, HD)
    keys_t[:HD] = arrived[:, 0].reshape(span, HD).T
    values_t[...] = arrived[:, 1].reshape(span, HD).T
    feature = lax.broadcasted_iota(jnp.int32, (HD, span), 0)
    prompt_live = jnp.broadcast_to(column(stats[:8], 2 * heads), (8, HD))[:1]
    prompt_live = jnp.concatenate([prompt_live] * (span // HD), axis=1)
    place = lax.broadcasted_iota(jnp.int32, (1, span), 1).astype(f32)
    barred = jnp.where(place >= prompt_live, MASKED, 0.0)
    keys_t[HD:] = jnp.where(feature == HD - 1, barred, keys_t[:HD].astype(f32)).astype(bf16)
    scores, slopes = (scores0, scores1), (slopes0, slopes1)
    grads, factors, terms = (grads0, grads1), (factors0, factors1), (terms0, terms1)
    query_sums, key_sums, value_sums = [], [], []
    tiles = span // TILE

    def columns(head):
        return slice(head * HD, (head + 1) * HD)

    def product(head, at, query):
        slot, part = head % 2, slice(at % tiles * TILE, (at % tiles + 1) * TILE)
        if at < tiles:
            scores[slot][:, part] = dot(query, keys_t[:, part], NN)
        else:
            slopes[slot][:, part] = dot(outs[:, columns(head)], values_t[:, part], NN)

    def softmax(head, at):
        slot, rows = head % 2, slice(at * ROWS, (at + 1) * ROWS)
        own_top, own_delta = (column(stats[rows], n * heads + head) for n in range(2))
        score = scores[slot][rows]
        top = jnp.maximum(jnp.max(score, 1, keepdims=True), own_top)
        prob = jnp.exp2(score - top)
        share = jnp.exp2(own_top - top)
        slope = slopes[slot][rows]
        inverse = 1.0 / (jnp.sum(prob, 1, keepdims=True) + share)
        delta = (jnp.sum(prob * slope, 1, keepdims=True) + own_delta * share) * inverse
        grads[slot][rows] = (prob * (slope - delta)).astype(bf16)
        factor = inverse * scale
        factors[slot][rows] = jnp.broadcast_to(factor, (ROWS, HD))
        own_factor = factor * share
        apart = own_delta - delta
        term = sloped[head, rows].astype(f32) + apart * plain[head, rows].astype(f32)
        terms[slot][rows] = term * own_factor
        by_query = apart * own_factor
        by_out = share * inverse
        key_sums.append(by_query * queries[rows, columns(head)].astype(f32))
        value_sums.append(by_out * outs[rows, columns(head)].astype(f32))
        for n, value in enumerate((top, inverse, delta)):
            final[rows, n * heads + head : n * heads + head + 1] = value

    def gradient(head, at, total):
        slot = head % 2
        if at < tiles:
            part = slice(at * TILE, (at + 1) * TILE)
            term = dot(grads[slot][:, part], keys[part], NN)
            return term if total is None else total + term
        total = total * factors[slot][...] + terms[slot][...]
        dq_ref[:, columns(head)] = total.astype(bf16)
        query_sums.append(jnp.sum(total, 0, keepdims=True))
        return total

    query = two_parts(queries[:, columns(0)])
    for at in range(2 * tiles):
        product(0, at, query)
    chunks = tokens // ROWS
    for head in range(heads):
        if head + 1 < heads:
            query = two_parts(queries[:, columns(head + 1)])
        total, done, made = None, 0, 0
        for chunk in range(chunks):
            while head + 1 < heads and made < 2 * tiles * (chunk + 1) // chunks:
                product(head + 1, made, query)
                made += 1
            while head > 0 and done < (tiles + 1) * (chunk + 1) // chunks:
                total = gradient(head - 1, done, total)
                done += 1
            softmax(head, chunk)
    total = None
    for at in range(tiles + 1):
        total = gradient(heads - 1, at, total)
    last = [jnp.sum(sum(rows), 0, keepdims=True) for rows in (key_sums, value_sums)]
    block = in_halves(query_sums + last).astype(bf16)
    for peer in range(message.shape[0]):
        message[peer] = block


def finish_kernel(
    lens, queries, outs, own, final, dq, dq_out, dkv_ref, token, keys_two, causal, sem
):
    bf16 = jnp.bfloat16
    copy = pltpu.make_async_copy(dq, dq_out, sem)
    copy.start()
    heads = queries.shape[1] // HD
    fill_own(lens[0], own[0], keys_two, causal)
    grad_keys = grad_values = None
    for head in range(heads):
        columns = slice(head * HD, (head + 1) * HD)
        top, inverse, delta = (column(final[...], n * heads + head) for n in range(3))
        query, grad = queries[:, columns], outs[:, columns]
        score = dot(two_parts(query), keys_two[...], NT) + causal[...]
        prob = jnp.exp2(score - top) * inverse
        mine = (prob * (dot(grad, own[1], NT) - delta) * (1.0 / math.sqrt(HD))).astype(bf16)
        by_key = dot(mine, query, TN)
        by_value = dot(prob.astype(bf16), grad, TN)
        grad_keys = by_key if head == 0 else grad_keys + by_key
        grad_values = by_value if head == 0 else grad_values + by_value
    dkv_ref[0] = grad_keys.astype(bf16)
    dkv_ref[1] = grad_values.astype(bf16)
    token[...] = jnp.zeros_like(token)
    copy.wait()


def steer_kernel(sums, w_query, w_kv, token, message):
    del token
    total = summed(sums)
    heads = w_query.shape[1] // HD
    chunks = [chunk_of(total, chunk, heads + 2) for chunk in range(heads + 2)]
    part = dot(in_thirds(jnp.concatenate(chunks[:heads], axis=1)), w_query[...], NT)
    for c in range(2):
        part = part + dot(in_thirds(chunks[heads + c]), w_kv[c], NT)
    row = jnp.sum(part, 0, keepdims=True)
    for peer in range(message.shape[0]):
        message[peer] = row


def shards(
    q_base,
    kv_base,
    cotangent,
    steering,
    w_query,
    w_kv,
    prompt_cache,
    prompt_ids,
    dialogue_lens,
    prompt_lens,
):
    dp = lax.axis_size("dp")
    tensor = lax.axis_size("tensor")
    f32 = jnp.float32
    tokens, width = q_base.shape
    positions = prompt_cache.shape[2]
    half_width = (width + 2 * HD) // 2
    bf16 = jnp.bfloat16
    message = pl.pallas_call(
        project_kernel,
        out_shape=jax.ShapeDtypeStruct((dp, 2, half_width + HD), jnp.int16),
        in_specs=[SMEM, HBM, HBM, HBM],
        out_specs=VMEM,
        scratch_shapes=[
            pltpu.VMEM((1, steering.shape[0]), f32),
            pltpu.VMEM(w_query.shape, bf16),
            pltpu.VMEM(w_kv.shape, bf16),
            pltpu.SemaphoreType.DMA((3,)),
        ],
        compiler_params=pltpu.CompilerParams(vmem_limit_bytes=63 * 2**20),
        name="project",
    )(prompt_ids, steering.reshape(1, -1), w_query, w_kv)
    shares = lax.all_to_all(message, "dp", 0, 0, tiled=True)
    outgoing = pl.pallas_call(
        pick_kernel,
        out_shape=jax.ShapeDtypeStruct((dp, 2, positions, HD), bf16),
        in_specs=[VMEM, VMEM],
        out_specs=HBM,
        scratch_shapes=[
            pltpu.VMEM((2, 1, HD), jnp.int32),
            pltpu.SMEM((2, 1, HD), jnp.int32),
            pltpu.SemaphoreType.DMA((3,)),
        ],
        compiler_params=PARAMS,
        name="pick",
    )(shares, prompt_cache)
    arrived = lax.all_to_all(outgoing, "dp", 0, 0, tiled=True)
    heads = width // HD
    span = dp * positions
    by_head = jax.ShapeDtypeStruct((heads, tokens, HD), bf16)
    by_row = jax.ShapeDtypeStruct((tokens, HD), f32)
    own_scratch = [pltpu.VMEM((tokens, 2 * HD), bf16), pltpu.VMEM((tokens, tokens), f32)]
    queries, outs, own = pl.pallas_call(
        shift_kernel,
        out_shape=(
            jax.ShapeDtypeStruct((tokens, width), bf16),
            jax.ShapeDtypeStruct((tokens, width), bf16),
            jax.ShapeDtypeStruct((2, tokens, HD), bf16),
        ),
        in_specs=[SMEM, VMEM, VMEM, VMEM, VMEM, HBM],
        out_specs=(VMEM,) * 3,
        compiler_params=PARAMS,
        name="shift",
    )(dialogue_lens, shares, q_base, kv_base, cotangent, outgoing)
    stats, sloped, plain = pl.pallas_call(
        prepare_kernel,
        out_shape=(by_row, by_head, by_head),
        in_specs=[SMEM, SMEM, SMEM, VMEM, VMEM, VMEM],
        out_specs=(VMEM,) * 3,
        scratch_shapes=own_scratch,
        compiler_params=PARAMS,
        name="prepare",
    )(prompt_ids, prompt_lens, dialogue_lens, queries, outs, own)
    held_grad, message, final = pl.pallas_call(
        attend_kernel,
        out_shape=(
            jax.ShapeDtypeStruct(q_base.shape, bf16),
            jax.ShapeDtypeStruct((dp, 2, half_width), bf16),
            by_row,
        ),
        in_specs=[VMEM] * 6,
        out_specs=(VMEM, VMEM, VMEM),
        scratch_shapes=[
            pltpu.VMEM((span, HD), bf16),
            pltpu.VMEM((2 * HD, span), bf16),
            pltpu.VMEM((HD, span), bf16),
        ]
        + [
            pltpu.VMEM((tokens, columns), kind)
            for columns, kind in ((span, f32), (span, f32), (span, bf16), (HD, f32), (HD, f32))
            for slot in range(2)
        ],
        compiler_params=PARAMS,
        name="attend",
    )(arrived, queries, outs, stats, sloped, plain)
    query_grad, kv_grad, token = pl.pallas_call(
        finish_kernel,
        out_shape=(
            jax.ShapeDtypeStruct(q_base.shape, bf16),
            jax.ShapeDtypeStruct(kv_base.shape, bf16),
            jax.ShapeDtypeStruct((8, HD), f32),
        ),
        in_specs=[SMEM] + [VMEM] * 5,
        out_specs=(HBM, VMEM, VMEM),
        scratch_shapes=own_scratch + [pltpu.SemaphoreType.DMA],
        compiler_params=PARAMS,
        name="finish",
    )(dialogue_lens, queries, outs, own, final, held_grad)
    sums = lax.all_to_all(message, "dp", 0, 0, tiled=True)
    message = pl.pallas_call(
        steer_kernel,
        out_shape=jax.ShapeDtypeStruct((tensor, 1, steering.shape[0]), f32),
        in_specs=[VMEM, VMEM, VMEM, VMEM],
        out_specs=VMEM,
        compiler_params=PARAMS,
        name="steer",
    )(sums, w_query, w_kv, token)
    parts = lax.all_to_all(message, "tensor", 0, 0, tiled=True)
    return (query_grad, kv_grad, jnp.sum(parts, axis=(0, 1)))


def solution(mesh):
    placed = (
        P("dp", "tensor"),
        P(None, "dp", "tensor"),
        P("dp", "tensor"),
        P("dp"),
        P("dp", "tensor"),
        P(None, "dp", "tensor"),
        P(None, None, "dp", "tensor"),
        P("dp"),
        P("dp"),
        P(),
    )
    return jax.shard_map(
        shards,
        mesh=mesh,
        in_specs=placed,
        out_specs=(P("dp", "tensor"), P(None, "dp", "tensor"), P("dp")),
        check_vma=False,
    )
```
